512 devices in a mesh: dp: 4 (over z_lo), tm: 16 (over x, z_hi), expert: 8 (over y, core).
Axes of the slice: x: 4, y: 4, z: 16 (z_hi: 4, z_lo: 4; z = z_hi * 4 + z_lo), core: 2. Of those that a mesh axis runs over, the one named last changes fastest.
Arguments:
- decoder_in: bfloat16 [4, 16384, 2048], P('dp', ('tm', 'expert')), may hold values from -6 to 6
- enc_keys: bfloat16 [4, 16384, 2048], P('dp', ('tm', 'expert')), may hold values from -4 to 4
- enc_values: bfloat16 [4, 16384, 2048], P('dp', ('tm', 'expert')), may hold values from -4 to 4
- win_start: int32 [4, 16384], P('dp', ('tm', 'expert')), may hold values from 0 to 16383, as said below
- win_end: int32 [4, 16384], P('dp', ('tm', 'expert')), may hold values from 1 to 16384, as said below
- routes: int32 [4, 16384, 2], P('dp', ('tm', 'expert')), may hold values from 0 to 31, as said below
- gate_probs: float32 [4, 16384, 2], P('dp', ('tm', 'expert')), may hold values from 0.1 to 1
- w_up: bfloat16 [8, 2048, 2048], P('expert', 'tm', 'dp'), may hold values from -0.125 to 0.125
- w_down: bfloat16 [8, 2048, 2048], P('expert', 'dp', 'tm'), may hold values from -0.09375 to 0.09375
- cotangent: bfloat16 [4, 16384, 2048], P('dp', ('tm', 'expert')), may hold values from -6 to 6
Outputs:
- block_out: bfloat16 [4, 16384, 2048], P('dp', ('tm', 'expert'))
- grad_in: bfloat16 [4, 16384, 2048], P('dp', ('tm', 'expert'))
- grad_keys: bfloat16 [4, 16384, 2048], P('dp', ('tm', 'expert'))
- grad_values: bfloat16 [4, 16384, 2048], P('dp', ('tm', 'expert'))
The draws below stay inside these ranges and needn't reach their ends.
Inputs may be any that keep to these rules, and one draw needn't show every extreme that they name: `win_start`: starts never fall along the tokens of a recording, and each token's window holds its own position and no frame more than 16 positions before the first token of its block of 128; in every draw and recording some token's window starts exactly 16 frames before its block. `win_end`: ends never fall along the tokens of a recording and lie after the token's own position, at most 16 frames past the last token of its block of 128; in every draw and recording some token's window ends exactly 16 frames past its block. `routes`: the two ids of a token differ. In each aligned block of 128 tokens any id below 4 is named at most 10 times; in every draw, for every recording and every index of tm, one id below 4 is named exactly 10 times in each of the 8 blocks of that index.
All inputs are finite; a program needn't handle non-finite values.
Results may differ from the reference program's by a relative error of at most 0.0063.
Values may be sent and summed in bfloat16 or wider, within the bound.
No kernel may reach another device: no remote copies, remote signals or barrier semaphores. Data moves between devices by JAX's collectives and lax.ppermute only.
A program may use at most 64 MiB of HBM per device.

```python
import math
import jax
import jax.numpy as jnp
from jax import lax

HEADS = 16
HD = 128
D = 2048
FF = 4096
TOKENS_PER_UNIT = 128
HALO = 16
SLOT_LIMIT = 10
PASS_EXPERTS = 4
ROUTED = 32
RECS = 4
TOKENS = 16384
FRAMES = 16384


def window_bounds(key):
    key = jax.random.fold_in(key, 5)
    key_back, key_ahead, key_first, key_last = jax.random.split(key, 4)
    blocks = TOKENS // TOKENS_PER_UNIT
    back_reach = jax.random.randint(key_back, (RECS, TOKENS), 0, HALO + 1)
    ahead_reach = jax.random.randint(key_ahead, (RECS, TOKENS), 0, HALO + 1)
    first_token = jax.random.randint(key_first, (RECS, 1), 1, blocks) * TOKENS_PER_UNIT
    last_token = jax.random.randint(key_last, (RECS, 1), 1, blocks) * TOKENS_PER_UNIT - 1
    position = jnp.arange(TOKENS, dtype=jnp.int32)[None, :]
    back_reach = jnp.where((position >= first_token - HALO) & (position <= first_token), HALO, back_reach)
    ahead_reach = jnp.where((position >= last_token) & (position <= last_token + HALO), HALO, ahead_reach)
    starts = jnp.maximum(lax.cummax(position - back_reach, axis=1), 0)
    ends = jnp.minimum(lax.cummin(position + 1 + ahead_reach, axis=1, reverse=True), TOKENS)
    return (starts.astype(jnp.int32), ends.astype(jnp.int32))


def draw_win_start(key, part):
    return window_bounds(key)[0]


def draw_win_end(key, part):
    return window_bounds(key)[1]


def draw_routes(key, part):
    key = jax.random.fold_in(key, 11)
    blocks = RECS * TOKENS // TOKENS_PER_UNIT
    group_size = 2 * PASS_EXPERTS
    groups = blocks // group_size
    key_full, key_load, key_perm, key_swap = jax.random.split(key, 4)
    full_expert = jax.random.randint(key_full, (groups,), 0, PASS_EXPERTS)
    whole_block = jnp.repeat(full_expert, group_size)
    expert_loads = jax.random.randint(key_load, (blocks, PASS_EXPERTS), max(1, SLOT_LIMIT // 2), SLOT_LIMIT + 1)
    pending_sends = jnp.where(jnp.arange(PASS_EXPERTS)[None, :] == whole_block[:, None], SLOT_LIMIT, expert_loads)
    still_left = 2 * TOKENS_PER_UNIT - jnp.sum(pending_sends, axis=1)
    others = ROUTED - PASS_EXPERTS
    base_count = still_left // others
    extra_count = (jnp.arange(others)[None, :] < (still_left % others)[:, None]).astype(jnp.int32)
    beyond_window = base_count[:, None] + extra_count
    expert_counts = jnp.concatenate([pending_sends, beyond_window], axis=1)
    bounds = jnp.cumsum(expert_counts, axis=1)
    position = jnp.arange(2 * TOKENS_PER_UNIT, dtype=jnp.int32)
    labels = jnp.sum((bounds[:, None, :] <= position[None, :, None]).astype(jnp.int32), axis=2)
    pairs = labels.reshape(blocks, 2, TOKENS_PER_UNIT).transpose(0, 2, 1)
    perm_keys = jax.random.split(key_perm, blocks)
    orders = jax.vmap(lambda key_one: jax.random.permutation(key_one, TOKENS_PER_UNIT))(perm_keys)
    pairs = jnp.take_along_axis(pairs, orders[:, :, None], axis=1)
    swapped = jax.random.randint(key_swap, (blocks, TOKENS_PER_UNIT, 1), 0, 2)
    pairs = jnp.where(swapped == 1, pairs[:, :, ::-1], pairs)
    return pairs.reshape(RECS, TOKENS, 2).astype(jnp.int32)


def level_of(own_key, dims, cuts, low, largest):
    gain, own = 1.0, jax.random.fold_in(own_key, 6)
    for axis_at, shards_of in cuts:
        draws = jnp.exp(jax.random.uniform(jax.random.fold_in(own, axis_at), (shards_of,), jnp.float32, low / len(cuts), largest / len(cuts)))
        gain = gain * jnp.repeat(draws, dims[axis_at] // shards_of).reshape([-1 if axis == axis_at else 1 for axis in range(len(dims))])
    return gain


def gaussian(own_key, extent, scale, most, cuts=(), kind=jnp.bfloat16):
    loudness = level_of(own_key, extent, cuts, -0.22, 0.18) if cuts else 1.0
    result = jax.random.normal(own_key, extent, jnp.float32) * scale * loudness
    return jnp.minimum(jnp.maximum(result, -most), most).astype(kind)


def setup_inputs(seed: int = 0) -> dict:
    streams_of = jax.random.split(jax.random.key(seed), 11)
    decoder_in = gaussian(streams_of[0], (RECS, TOKENS, D), 1.0, 6.0, ((0, 4), (1, 128)))
    enc_keys = gaussian(streams_of[1], (RECS, FRAMES, D), 1.0, 4.0, ((0, 4), (1, 128)))
    enc_values = gaussian(streams_of[2], (RECS, FRAMES, D), 1.0, 4.0, ((0, 4), (1, 128)))
    win_start = draw_win_start(jax.random.fold_in(streams_of[10], 71), 0)
    win_end = draw_win_end(jax.random.fold_in(streams_of[10], 71), 0)
    routes = draw_routes(jax.random.fold_in(streams_of[10], 71), 0)
    gate_probs = jnp.clip(0.1 + 0.9 * jax.random.uniform(streams_of[6], (RECS, TOKENS, 2), jnp.float32) ** level_of(streams_of[6], (RECS, TOKENS, 2), ((0, 4), (1, 128)), -0.2, 0.2), 0.1, 1.0)
    w_up = gaussian(streams_of[7], (2 * PASS_EXPERTS, D, FF // 2), D ** -0.5, 0.125, ((0, 8), (1, 16), (2, 4)))
    w_down = gaussian(streams_of[8], (2 * PASS_EXPERTS, FF // 2, D), FF ** -0.5, 0.09375, ((0, 8), (1, 4), (2, 16)))
    cotangent = gaussian(streams_of[9], (RECS, TOKENS, D), 1.0, 6.0, ((0, 4), (1, 128)))
    return {"decoder_in": decoder_in, "enc_keys": enc_keys, "enc_values": enc_values, "win_start": win_start, "win_end": win_end, "routes": routes, "gate_probs": gate_probs, "w_up": w_up, "w_down": w_down, "cotangent": cotangent}


NORM_EPS = 1e-06
ROOT_HALF = 1.0 / math.sqrt(2.0)
INV_ROOT_TWOPI = 1.0 / math.sqrt(2.0 * math.pi)

def rounded(value):
    return lax.optimization_barrier(value.astype(jnp.bfloat16)).astype(jnp.float32)

def gelu_parts(pre_act):
    gauss_cdf = 0.5 * (1.0 + jax.scipy.special.erf(pre_act * ROOT_HALF))
    slope = gauss_cdf + pre_act * jnp.exp(-0.5 * pre_act * pre_act) * INV_ROOT_TWOPI
    return (pre_act * gauss_cdf, slope)

def attend(piece_in, piece_keys, piece_values, starts, ends, first_frame):
    tok_rows = piece_in.shape[0]
    key_span = piece_keys.shape[0]
    heads_in = piece_in.astype(jnp.float32).reshape(tok_rows, HEADS, HD)
    scale_q = lax.rsqrt(lax.optimization_barrier(jnp.mean(heads_in * heads_in, axis=-1, keepdims=True)) + NORM_EPS)
    normed = heads_in * scale_q
    query_low = rounded(normed)
    key_heads = piece_keys.astype(jnp.float32).reshape(key_span, HEADS, HD)
    val_heads = piece_values.astype(jnp.float32).reshape(key_span, HEADS, HD)
    scores = jnp.einsum('thd,fhd->htf', query_low, key_heads) * (1.0 / math.sqrt(HD))
    frame = first_frame + jnp.arange(key_span, dtype=jnp.int32)
    inside = (frame[None, :] >= starts[:, None]) & (frame[None, :] < ends[:, None])
    weights = jnp.exp(scores) * inside[None].astype(jnp.float32)
    att_probs = weights / lax.optimization_barrier(jnp.sum(weights, axis=-1, keepdims=True))
    probs_low = rounded(att_probs)
    context = jnp.einsum('htf,fhd->thd', probs_low, val_heads).reshape(tok_rows, HEADS * HD)
    return (context, (scale_q, normed, query_low, key_heads, val_heads, att_probs, probs_low))

def attend_back(grad_hidden, saved):
    scale_q, normed, query_low, key_heads, val_heads, att_probs, probs_low = saved
    tok_rows = grad_hidden.shape[0]
    key_span = key_heads.shape[0]
    grad_low = rounded(grad_hidden).reshape(tok_rows, HEADS, HD)
    grad_probs = jnp.einsum('thd,fhd->htf', grad_low, val_heads)
    grad_scores = att_probs * (grad_probs - lax.optimization_barrier(jnp.sum(att_probs * grad_probs, axis=-1, keepdims=True))) * (1.0 / math.sqrt(HD))
    scores_low = rounded(grad_scores)
    grad_query = jnp.einsum('htf,fhd->thd', scores_low, key_heads)
    grad_key = jnp.einsum('htf,thd->fhd', scores_low, query_low).reshape(key_span, HEADS * HD)
    grad_value = jnp.einsum('htf,thd->fhd', probs_low, grad_low).reshape(key_span, HEADS * HD)
    grad_piece = scale_q * (grad_query - normed * lax.optimization_barrier(jnp.mean(grad_query * normed, axis=-1, keepdims=True)))
    return (grad_piece.reshape(tok_rows, HEADS * HD), grad_key, grad_value)

def slot_tables(route_ids, gates):
    blocks = route_ids.shape[0]
    flat_ids = route_ids.reshape(blocks, 2 * TOKENS_PER_UNIT)
    member = (flat_ids[:, :, None] == jnp.arange(PASS_EXPERTS, dtype=jnp.int32)[None, None, :]).astype(jnp.int32)
    earlier_count = jnp.cumsum(member, axis=1) - member
    slot_place = member[:, :, :, None] * (earlier_count[:, :, :, None] == jnp.arange(SLOT_LIMIT, dtype=jnp.int32)[None, None, None, :]).astype(jnp.int32)
    slot_place = slot_place.astype(jnp.float32).reshape(blocks, TOKENS_PER_UNIT, 2, PASS_EXPERTS * SLOT_LIMIT)
    slot_table = lax.optimization_barrier(jnp.sum(slot_place, axis=2))
    weighted = lax.optimization_barrier(jnp.sum(slot_place * gates[:, :, :, None], axis=2))
    return (slot_table, weighted)

def expert_forward(packed):
    rows_in, up_one, down_one = packed
    pre_act = jnp.dot(rows_in, up_one, preferred_element_type=jnp.float32)
    gelu_val, gelu_slope = gelu_parts(pre_act)
    block_size = FF // (2 * RECS)
    gelu_low = rounded(gelu_val).reshape(-1, 2 * RECS, block_size)
    partial_value = jnp.einsum('mnk,nkd->nmd', gelu_low, down_one.astype(jnp.float32).reshape(2 * RECS, block_size, D))
    return (lax.optimization_barrier(jnp.sum(rounded(partial_value), axis=0)), gelu_slope)

def expert_backward(packed):
    grads_in, gelu_slope, up_one, down_one = packed
    block_size = FF // (2 * RECS)
    grad_gelu = jnp.einsum('md,kd->mk', grads_in, down_one.astype(jnp.float32))
    grad_act = rounded(grad_gelu * gelu_slope).reshape(-1, 2 * RECS, block_size)
    partial_value = jnp.einsum('mnk,dnk->nmd', grad_act, up_one.astype(jnp.float32).reshape(D, 2 * RECS, block_size))
    return lax.optimization_barrier(jnp.sum(rounded(partial_value), axis=0))

def one_recording(decoder_in, enc_keys, enc_values, win_start, win_end, routes, gate_probs, up_full, down_full, cotangent):
    blocks = TOKENS // TOKENS_PER_UNIT
    key_span = TOKENS_PER_UNIT + 2 * HALO
    pad_keys = jnp.pad(enc_keys, ((HALO, HALO), (0, 0)))
    pad_values = jnp.pad(enc_values, ((HALO, HALO), (0, 0)))

    def block_pieces(block_index):
        low_row = block_index * TOKENS_PER_UNIT
        piece_in = lax.dynamic_slice_in_dim(decoder_in, low_row, TOKENS_PER_UNIT, 0)
        piece_keys = lax.dynamic_slice_in_dim(pad_keys, low_row, key_span, 0)
        piece_values = lax.dynamic_slice_in_dim(pad_values, low_row, key_span, 0)
        starts = lax.dynamic_slice_in_dim(win_start, low_row, TOKENS_PER_UNIT, 0)
        ends = lax.dynamic_slice_in_dim(win_end, low_row, TOKENS_PER_UNIT, 0)
        return attend(piece_in, piece_keys, piece_values, starts, ends, low_row - HALO)

    def forward_block(block_index):
        return block_pieces(block_index)[0]
    block_ids = jnp.arange(blocks, dtype=jnp.int32)
    contexts = lax.map(forward_block, block_ids).reshape(TOKENS, D)
    hidden = decoder_in.astype(jnp.float32) + contexts
    scale_h = lax.rsqrt(lax.optimization_barrier(jnp.mean(hidden * hidden, axis=-1, keepdims=True)) + NORM_EPS)
    normed_h = hidden * scale_h
    normed_low = rounded(normed_h)
    slot_table, weighted = slot_tables(routes.reshape(blocks, TOKENS_PER_UNIT, 2), gate_probs.reshape(blocks, TOKENS_PER_UNIT, 2))
    slot_in = jnp.einsum('nts,ntd->nsd', slot_table, normed_low.reshape(blocks, TOKENS_PER_UNIT, D))
    slot_in = slot_in.reshape(blocks, PASS_EXPERTS, SLOT_LIMIT, D).transpose(1, 0, 2, 3).reshape(PASS_EXPERTS, blocks * SLOT_LIMIT, D)
    slot_out, slopes = lax.map(expert_forward, (slot_in.astype(jnp.bfloat16), up_full, down_full))
    slot_out = slot_out.reshape(PASS_EXPERTS, blocks, SLOT_LIMIT, D).transpose(1, 0, 2, 3).reshape(blocks, PASS_EXPERTS * SLOT_LIMIT, D)
    moe_mixed = jnp.einsum('nts,nsd->ntd', weighted, slot_out, precision=lax.Precision.HIGHEST).reshape(TOKENS, D)
    block_out = (hidden + moe_mixed).astype(jnp.bfloat16)
    grad_out = cotangent.astype(jnp.float32)
    slot_grad = rounded(jnp.einsum('nts,ntd->nsd', weighted, grad_out.reshape(blocks, TOKENS_PER_UNIT, D), precision=lax.Precision.HIGHEST))
    slot_grad = slot_grad.reshape(blocks, PASS_EXPERTS, SLOT_LIMIT, D).transpose(1, 0, 2, 3).reshape(PASS_EXPERTS, blocks * SLOT_LIMIT, D)
    slot_back = lax.map(expert_backward, (slot_grad, slopes, up_full, down_full))
    slot_back = slot_back.reshape(PASS_EXPERTS, blocks, SLOT_LIMIT, D).transpose(1, 0, 2, 3).reshape(blocks, PASS_EXPERTS * SLOT_LIMIT, D)
    grad_norm = jnp.einsum('nts,nsd->ntd', slot_table, slot_back, precision=lax.Precision.HIGHEST).reshape(TOKENS, D)
    grad_hidden = grad_out + scale_h * (grad_norm - normed_h * lax.optimization_barrier(jnp.mean(grad_norm * normed_h, axis=-1, keepdims=True)))

    def backward_block(carry, block_index):
        grad_key_all, grad_value_all = carry
        low_row = block_index * TOKENS_PER_UNIT
        saved = block_pieces(block_index)[1]
        grad_piece = lax.dynamic_slice_in_dim(grad_hidden, low_row, TOKENS_PER_UNIT, 0)
        grad_in_piece, grad_key, grad_value = attend_back(grad_piece, saved)
        grad_key_all = lax.dynamic_update_slice_in_dim(grad_key_all, lax.dynamic_slice_in_dim(grad_key_all, low_row, key_span, 0) + grad_key, low_row, 0)
        grad_value_all = lax.dynamic_update_slice_in_dim(grad_value_all, lax.dynamic_slice_in_dim(grad_value_all, low_row, key_span, 0) + grad_value, low_row, 0)
        return ((grad_key_all, grad_value_all), grad_in_piece)
    zero_grads = jnp.zeros((TOKENS + 2 * HALO, D), jnp.float32)
    (grad_key_all, grad_value_all), grad_pieces = lax.scan(backward_block, (zero_grads, zero_grads), block_ids)
    grad_in = (grad_hidden + grad_pieces.reshape(TOKENS, D)).astype(jnp.bfloat16)
    grad_keys = grad_key_all[HALO:HALO + TOKENS].astype(jnp.bfloat16)
    grad_values = grad_value_all[HALO:HALO + TOKENS].astype(jnp.bfloat16)
    return (block_out, grad_in, grad_keys, grad_values)

def reference(decoder_in, enc_keys, enc_values, win_start, win_end, routes, gate_probs, w_up, w_down, cotangent):
    up_full = w_up.reshape(PASS_EXPERTS, 2, D, FF // 2).transpose(0, 2, 1, 3).reshape(PASS_EXPERTS, D, FF)
    down_full = w_down.reshape(PASS_EXPERTS, FF, D)
    results = []
    for record in range(RECS):
        results.append(one_recording(decoder_in[record], enc_keys[record], enc_values[record], win_start[record], win_end[record], routes[record], gate_probs[record], up_full, down_full, cotangent[record]))
    return (jnp.stack([item[0] for item in results]), jnp.stack([item[1] for item in results]), jnp.stack([item[2] for item in results]), jnp.stack([item[3] for item in results]))
```

```python
import math

import jax
import jax.numpy as jnp
from jax import lax
from jax.experimental import pallas as pl
from jax.experimental.pallas import tpu as pltpu
from jax.sharding import Mesh, PartitionSpec as P

HEADS = 16
HD = 128
HALO = 16
SLOT_LIMIT = 10
EXPERTS = 4
SLOTS = EXPERTS * SLOT_LIMIT
LANES = 128

NORM_EPS = 1e-06
ROOT_HALF = 1.0 / math.sqrt(2.0)
INV_ROOT_TWOPI = 1.0 / math.sqrt(2.0 * math.pi)
INV_ROOT_HD = 1.0 / math.sqrt(HD)

BF = jnp.bfloat16
F32 = jnp.float32
VMEM_LIMIT = 56 * 1024 * 1024

NT = (((1,), (1,)), ((), ()))
TN = (((0,), (0,)), ((), ()))


def mm(a, b, dims=(((1,), (0,)), ((), ()))):
    return lax.dot_general(a, b, dims, preferred_element_type=F32)


def call(body, outs, args, scratch=(), flops=10**8, aliases=None):
    nbytes = sum(math.prod(a.shape) * a.dtype.itemsize for a in args)
    nbytes += sum(math.prod(o.shape) * o.dtype.itemsize for o in outs)
    return pl.pallas_call(
        body,
        out_shape=outs,
        in_specs=[pl.BlockSpec(memory_space=pltpu.VMEM)] * len(args),
        out_specs=[pl.BlockSpec(memory_space=pltpu.VMEM)] * len(outs),
        scratch_shapes=list(scratch),
        input_output_aliases=aliases or {},
        compiler_params=pltpu.CompilerParams(vmem_limit_bytes=VMEM_LIMIT),
        cost_estimate=pl.CostEstimate(flops=flops, bytes_accessed=nbytes, transcendentals=0),
    )(*args)


def shaped(shape, dtype):
    return jax.ShapeDtypeStruct(shape, dtype)


def slot_table(routes_ref):
    tokens = routes_ref.shape[1]
    first, second = routes_ref[0:1, :], routes_ref[1:2, :]
    slot = lax.broadcasted_iota(jnp.int32, (SLOTS, tokens), 0)
    expert = jnp.zeros_like(slot)
    for e in range(1, EXPERTS):
        expert = expert + (slot >= e * SLOT_LIMIT).astype(jnp.int32)
    rank = (slot - expert * SLOT_LIMIT).astype(F32)
    is_first = first == expert
    member = is_first | (second == expert)
    before = lax.broadcasted_iota(jnp.int32, (tokens, tokens), 0)
    after = lax.broadcasted_iota(jnp.int32, (tokens, tokens), 1)
    earlier = mm(
        jnp.where(member, 1.0, 0.0).astype(BF), jnp.where(before < after, 1.0, 0.0).astype(BF)
    )
    table = jnp.where(member & (earlier == rank), 1.0, 0.0)
    return table, is_first


def slot_gates(table, is_first, gates_ref):
    gate = jnp.where(is_first, gates_ref[0:1, :], gates_ref[1:2, :])
    return jnp.sum(table * gate, axis=1, keepdims=True)


def to_travel(rows, scratch, row_count, base=0):
    for c in range(rows.shape[1] // LANES):
        scratch[pl.ds(base + c, row_count, stride=16), :] = rows[:, c * LANES : (c + 1) * LANES]


def from_travel(scratch, row_count, c, base=0):
    return scratch[pl.ds(base + c, row_count, stride=16), :]


def scatter_slots(table, rows):
    high = rows.astype(BF)
    low = (rows - high.astype(F32)).astype(BF)
    table_low = table.astype(BF)
    return mm(table_low, high, TN) + mm(table_low, low, TN)


def grad_slots_kernel(routes, gates, cot, out, scratch):
    table, is_first = slot_table(routes)
    gate = slot_gates(table, is_first, gates)
    rows = mm(table.astype(BF), cot[...]) * gate
    to_travel(rows, scratch, SLOTS)
    sent = scratch[...].astype(BF)
    for d in range(out.shape[0]):
        out[d] = sent


def query_of(x):
    scale = lax.rsqrt(jnp.mean(x * x, axis=-1, keepdims=True) + NORM_EPS)
    return x * scale, scale


def attend_kernel(
    routes, bounds, dec, keys, values, halo_lo, halo_hi,
    sent, hidden, probs, k_all, v_all, scratch,
):
    tokens = dec.shape[0]
    span = tokens + 2 * HALO
    for all_ref, own, i in ((k_all, keys, 0), (v_all, values, 1)):
        all_ref[0:HALO, :] = halo_lo[i]
        all_ref[HALO : HALO + tokens, :] = own[...]
        all_ref[HALO + tokens : span, :] = halo_hi[i]
    frame = lax.broadcasted_iota(jnp.int32, (tokens, span), 1)
    inside = (frame >= bounds[:, 0:1]) & (frame < bounds[:, 1:2])
    square = jnp.zeros((tokens, 1), F32)
    for h in range(HEADS):
        cols = slice(h * HD, (h + 1) * HD)
        x = dec[:, cols].astype(F32)
        query = query_of(x)[0].astype(BF)
        scores = mm(query, k_all[:, cols], NT) * INV_ROOT_HD
        weights = jnp.where(inside, jnp.exp(scores), 0.0)
        att = weights / jnp.sum(weights, axis=-1, keepdims=True)
        probs[h] = att
        mixed = x + mm(att.astype(BF), v_all[:, cols])
        hidden[:, cols] = mixed
        square = square + jnp.sum(mixed * mixed, axis=-1, keepdims=True)
    scale_h = lax.rsqrt(square * (1.0 / (HEADS * HD)) + NORM_EPS)
    table = slot_table(routes)[0].astype(BF)
    rows = mm(table, (hidden[...] * scale_h).astype(BF))
    to_travel(rows, scratch, SLOTS)
    low = scratch[...].astype(BF)
    for d in range(sent.shape[0]):
        sent[d] = low


def rows_kernel(own, other, out, scratch):
    half = own.shape[0] // 16
    for i, ref in enumerate((own, other)):
        scratch[...] = ref[...].astype(F32)
        for c in range(out.shape[1] // LANES):
            out[i * half : (i + 1) * half, c * LANES : (c + 1) * LANES] = from_travel(
                scratch, half, c
            ).astype(BF)


def gelu_parts(pre_act):
    gauss_cdf = 0.5 * (1.0 + lax.erf(pre_act * ROOT_HALF))
    slope = gauss_cdf + pre_act * jnp.exp(-0.5 * pre_act * pre_act) * INV_ROOT_TWOPI
    return (pre_act * gauss_cdf, slope)


def send_halves(lhs, rhs_of, outs, scratches):
    half = lhs.shape[0] // 2
    for c in range(0, 16, 2):
        part = rhs_of(lhs, c)
        for i, scratch in enumerate(scratches):
            for k in range(2):
                scratch[pl.ds(c + k, half, stride=16), :] = part[
                    i * half : (i + 1) * half, k * LANES : (k + 1) * LANES
                ]
    for out, scratch in zip(outs, scratches):
        out[...] = scratch[...].astype(BF)


def expert_back_kernel(place, rows_in, rows_grad, *refs):
    pieces, (own, other, gelu, up, down, sc_own, sc_other) = refs[:-7], refs[-7:]
    assemble(place, pieces, up, down)
    pre_act = mm(rows_in[...], up[...])
    value, slope = gelu_parts(pre_act)
    gelu[...] = value.astype(BF)
    grad_act = (mm(rows_grad[...], down[...], NT) * slope).astype(BF)
    send_halves(
        grad_act,
        lambda lhs, c: mm(lhs, up[c * LANES : (c + 2) * LANES, :], NT),
        (own, other),
        (sc_own, sc_other),
    )


def expert_out_kernel(gelu, down, own, other, sc_own, sc_other):
    send_halves(
        gelu[...],
        lambda lhs, c: mm(lhs, down[:, c * LANES : (c + 2) * LANES]),
        (own, other),
        (sc_own, sc_other),
    )


def assemble(place, pieces, up, down):
    (whole,) = pieces
    block = LANES
    for tm in range(16):
        up[tm * block : (tm + 1) * block, :] = whole[tm, 0:block, :]
        for q in range(4):
            down[q * block : (q + 1) * block, tm * block : (tm + 1) * block] = whole[
                tm, block : 2 * block, q * block : (q + 1) * block
            ]


def slot_sum(back, scratch):
    total = back[0].astype(F32)
    for d in range(1, back.shape[0]):
        total = total + back[d].astype(F32)
    scratch[...] = total
    return jnp.concatenate([from_travel(scratch, SLOTS, c) for c in range(16)], axis=1)


def out_kernel(routes, gates, back, hidden, out, scratch):
    table, is_first = slot_table(routes)
    rows = slot_sum(back, scratch) * slot_gates(table, is_first, gates)
    out[...] = (hidden[...] + scatter_slots(table, rows)).astype(BF)


def attend_back_kernel(
    routes, back, cot, hidden, dec, probs, keys, values, halo_lo, halo_hi,
    grad_in, grad_k, grad_v, edge, send, k_all, v_all, scratch, grad_h,
):
    tokens = dec.shape[0]
    span = tokens + 2 * HALO
    for all_ref, own, i in ((k_all, keys, 0), (v_all, values, 1)):
        all_ref[0:HALO, :] = halo_lo[i]
        all_ref[HALO : HALO + tokens, :] = own[...]
        all_ref[HALO + tokens : span, :] = halo_hi[i]
    table, _ = slot_table(routes)
    grad_norm = scatter_slots(table, slot_sum(back, scratch))
    mixed = hidden[...]
    scale_h = lax.rsqrt(jnp.mean(mixed * mixed, axis=-1, keepdims=True) + NORM_EPS)
    normed = mixed * scale_h
    grad_h[...] = cot[...].astype(F32) + scale_h * (
        grad_norm - normed * jnp.mean(grad_norm * normed, axis=-1, keepdims=True)
    )
    for h in range(HEADS):
        cols = slice(h * HD, (h + 1) * HD)
        grad_hidden = grad_h[:, cols]
        grad_low = grad_hidden.astype(BF)
        att = probs[h]
        grad_probs = mm(grad_low, v_all[:, cols], NT)
        inner = jnp.sum(att * grad_probs, axis=-1, keepdims=True)
        scores_low = (att * (grad_probs - inner) * INV_ROOT_HD).astype(BF)
        query, scale_q = query_of(dec[:, cols].astype(F32))
        grad_query = mm(scores_low, k_all[:, cols])
        piece = scale_q * (
            grad_query - query * jnp.mean(grad_query * query, axis=-1, keepdims=True)
        )
        grad_in[:, cols] = (grad_hidden + piece).astype(BF)
        both = (
            mm(scores_low, query.astype(BF), TN),
            mm(att.astype(BF), grad_low, TN),
        )
        for i, (grad, ref) in enumerate(zip(both, (grad_k, grad_v))):
            ref[:, cols] = grad[HALO : HALO + tokens, :].astype(BF)
            edge[i, 0, :, cols] = grad[HALO : 2 * HALO, :]
            edge[i, 1, :, cols] = grad[tokens : HALO + tokens, :]
            send[0, i, :, cols] = grad[0:HALO, :].astype(BF)
            send[1, i, :, cols] = grad[HALO + tokens : span, :].astype(BF)


def shift(value, axis, step):
    count = lax.axis_size(axis)
    return lax.ppermute(value, axis, [(i, (i + step) % count) for i in range(count)])


def neighbours(tail, head):
    axes = ("x", "zh", "y", "core")
    count = lax.axis_size(axes)
    return (
        lax.ppermute(tail, axes, [(i, i + 1) for i in range(count - 1)]),
        lax.ppermute(head, axes, [(i + 1, i) for i in range(count - 1)]),
    )


def exchange(sent):
    shape = sent.shape
    got = lax.all_to_all(
        sent.reshape(-1, 160, LANES), ("dp", "y"), split_axis=0, concat_axis=0, tiled=True
    )
    return got.reshape(shape)


def gather_weights(up_local, down_local):
    turned = down_local.reshape(4, LANES, LANES).transpose(1, 0, 2).reshape(LANES, 4 * LANES)
    packed = jnp.concatenate([up_local, turned], axis=0)
    whole = lax.all_gather(packed, ("x", "zh"), axis=0, tiled=True)
    return (whole.reshape(16, 2 * LANES, 4 * LANES),)


def slot_rows(got):
    mine = got.reshape(-1, LANES)
    other = shift(mine, "core", 1)
    count = mine.shape[0]
    return call(
        rows_kernel,
        [shaped((2 * count // 16, 16 * LANES), BF)],
        (mine, other),
        scratch=[pltpu.VMEM((count, LANES), F32)],
    )[0]


def send_back(own, other):
    total = own.astype(F32) + shift(other, "core", 1).astype(F32)
    return exchange(total.astype(BF).reshape(4, EXPERTS * 160, LANES))


def shards(
    decoder_in, enc_keys, enc_values, win_start, win_end, routes, gate_probs, w_up, w_down, cotangent
):
    dec, keys, values, cot = decoder_in[0], enc_keys[0], enc_values[0], cotangent[0]
    tokens, feat = dec.shape
    span = tokens + 2 * HALO
    position = lax.axis_index(("x", "zh", "y", "core"))
    place = jnp.stack([lax.axis_index("x"), lax.axis_index("zh")]).astype(jnp.int32)
    bounds = jnp.stack([win_start[0], win_end[0]], axis=1) - (position * tokens - HALO)
    routes_t = routes[0].T
    gates_t = gate_probs[0].T

    pieces = gather_weights(w_up[0], w_down[0])
    halo_lo, halo_hi = neighbours(
        jnp.stack([keys[tokens - HALO :], values[tokens - HALO :]]),
        jnp.stack([keys[:HALO], values[:HALO]]),
    )

    travel = (4, EXPERTS * 160, LANES)
    (grad_sent,) = call(
        grad_slots_kernel,
        [shaped(travel, BF)],
        (routes_t, gates_t, cot),
        scratch=[pltpu.VMEM(travel[1:], F32)],
    )
    grad_rows = slot_rows(exchange(grad_sent))

    in_sent, hidden, probs = call(
        attend_kernel,
        [shaped(travel, BF), shaped((tokens, feat), F32), shaped((HEADS, tokens, span), F32)],
        (routes_t, bounds, dec, keys, values, halo_lo, halo_hi),
        scratch=[
            pltpu.VMEM((span, feat), BF),
            pltpu.VMEM((span, feat), BF),
            pltpu.VMEM(travel[1:], F32),
        ],
    )
    in_rows = slot_rows(exchange(in_sent))

    rows, units = in_rows.shape[0], 4 * LANES
    half = (rows // 2 * 16, LANES)
    back_own, back_other, gelu, up_full, down_full = call(
        expert_back_kernel,
        [
            shaped(half, BF),
            shaped(half, BF),
            shaped((rows, units), BF),
            shaped((feat, units), BF),
            shaped((units, feat), BF),
        ],
        (place, in_rows, grad_rows, *pieces),
        scratch=[pltpu.VMEM(half, F32), pltpu.VMEM(half, F32)],
    )
    back = send_back(back_own, back_other)
    value_own, value_other = call(
        expert_out_kernel,
        [shaped(half, BF), shaped(half, BF)],
        (gelu, down_full),
        scratch=[pltpu.VMEM(half, F32), pltpu.VMEM(half, F32)],
    )
    result = send_back(value_own, value_other)

    grad_in, grad_k, grad_v, edge, send = call(
        attend_back_kernel,
        [
            shaped((tokens, feat), BF),
            shaped((tokens, feat), BF),
            shaped((tokens, feat), BF),
            shaped((2, 2, HALO, feat), F32),
            shaped((2, 2, HALO, feat), BF),
        ],
        (routes_t, back, cot, hidden, dec, probs, keys, values, halo_lo, halo_hi),
        scratch=[
            pltpu.VMEM((span, feat), BF),
            pltpu.VMEM((span, feat), BF),
            pltpu.VMEM(travel[1:], F32),
            pltpu.VMEM((tokens, feat), F32),
        ],
    )
    from_lo, from_hi = neighbours(send[1], send[0])
    (block_out,) = call(
        out_kernel,
        [shaped((tokens, feat), BF)],
        (routes_t, gates_t, result, hidden),
        scratch=[pltpu.VMEM(travel[1:], F32)],
    )
    grads = []
    for i, grad in enumerate((grad_k, grad_v)):
        low = (edge[i, 0] + from_lo[i].astype(F32)).astype(BF)
        high = (edge[i, 1] + from_hi[i].astype(F32)).astype(BF)
        grad = lax.dynamic_update_slice(grad, low, (0, 0))
        grad = lax.dynamic_update_slice(grad, high, (tokens - HALO, 0))
        grads.append(grad)
    return (block_out[None], grad_in[None], grads[0][None], grads[1][None])


def solution(mesh):
    fine = Mesh(mesh.devices.reshape(4, 4, 4, 4, 2), ("dp", "x", "zh", "y", "core"))
    time = ("x", "zh", "y", "core")
    wide = P("dp", time, None)
    return jax.shard_map(
        shards,
        mesh=fine,
        in_specs=(
            wide,
            wide,
            wide,
            P("dp", time),
            P("dp", time),
            wide,
            wide,
            P(("y", "core"), ("x", "zh"), "dp"),
            P(("y", "core"), "dp", ("x", "zh")),
            wide,
        ),
        out_specs=(wide, wide, wide, wide),
        check_vma=False,
    )
```

```python
import math

import jax
import jax.numpy as jnp
from jax import lax
from jax.experimental import pallas as pl
from jax.experimental.pallas import tpu as pltpu
from jax.sharding import Mesh, PartitionSpec as P

HEADS = 16
HD = 128
HALO = 16
SLOT_LIMIT = 10
EXPERTS = 4
SLOTS = EXPERTS * SLOT_LIMIT
LANES = 128
TRAVEL_ROWS = SLOT_LIMIT * 16

NORM_EPS = 1e-06
ROOT_HALF = 1.0 / math.sqrt(2.0)
INV_ROOT_TWOPI = 1.0 / math.sqrt(2.0 * math.pi)
INV_ROOT_HD = 1.0 / math.sqrt(HD)

BF = jnp.bfloat16
F32 = jnp.float32
VMEM_LIMIT = 56 * 1024 * 1024

NT = (((1,), (1,)), ((), ()))
TN = (((0,), (0,)), ((), ()))


def mm(a, b, dims=(((1,), (0,)), ((), ()))):
    return lax.dot_general(a, b, dims, preferred_element_type=F32)


def call(body, outs, args, scratch=(), flops=10**8, scalars=0):
    nbytes = sum(math.prod(a.shape) * a.dtype.itemsize for a in args)
    nbytes += sum(math.prod(o.shape) * o.dtype.itemsize for o in outs)
    return pl.pallas_call(
        body,
        out_shape=outs,
        in_specs=[pl.BlockSpec(memory_space=pltpu.SMEM)] * scalars
        + [pl.BlockSpec(memory_space=pltpu.VMEM)] * (len(args) - scalars),
        out_specs=[pl.BlockSpec(memory_space=pltpu.VMEM)] * len(outs),
        scratch_shapes=list(scratch),
        compiler_params=pltpu.CompilerParams(vmem_limit_bytes=VMEM_LIMIT),
        cost_estimate=pl.CostEstimate(flops=flops, bytes_accessed=nbytes, transcendentals=0),
    )(*args)


def shaped(shape, dtype):
    return jax.ShapeDtypeStruct(shape, dtype)


def slot_table(routes_ref, stride=SLOT_LIMIT):
    tokens = routes_ref.shape[1]
    first, second = routes_ref[0:1, :], routes_ref[1:2, :]
    slot = lax.broadcasted_iota(jnp.int32, (EXPERTS * stride, tokens), 0)
    expert = jnp.zeros_like(slot)
    for e in range(1, EXPERTS):
        expert = expert + (slot >= e * stride).astype(jnp.int32)
    rank = (slot - expert * stride).astype(F32)
    is_first = first == expert
    member = is_first | (second == expert)
    before = lax.broadcasted_iota(jnp.int32, (tokens, tokens), 0)
    after = lax.broadcasted_iota(jnp.int32, (tokens, tokens), 1)
    earlier = mm(
        jnp.where(member, 1.0, 0.0).astype(BF), jnp.where(before < after, 1.0, 0.0).astype(BF)
    )
    table = jnp.where(member & (earlier == rank), 1.0, 0.0)
    return table, is_first


def slot_gates(table, is_first, gates_ref):
    gate = jnp.where(is_first, gates_ref[0:1, :], gates_ref[1:2, :])
    return jnp.sum(table * gate, axis=1, keepdims=True)


def from_travel(scratch, row_count, c, base=0):
    return scratch[pl.ds(base + c, row_count, stride=16), :]


def scatter_slots(table, rows):
    high = rows.astype(BF)
    low = (rows - high.astype(F32)).astype(BF)
    table_low = table.astype(BF)
    return mm(table_low, high, TN) + mm(table_low, low, TN)


def slots_to_travel(rows, scratch, kind):
    for e in range(EXPERTS):
        base = (2 * e + kind) * TRAVEL_ROWS
        for c in range(16):
            scratch[pl.ds(base + c, SLOT_LIMIT, stride=16), :] = rows[
                e * 16 : e * 16 + SLOT_LIMIT, c * LANES : (c + 1) * LANES
            ]


def query_of(x):
    scale = lax.rsqrt(jnp.mean(x * x, axis=-1, keepdims=True) + NORM_EPS)
    return x * scale, scale


def attend_kernel(
    routes, gates, bounds, dec, cot, keys, values, halo_lo, halo_hi,
    sent, hidden, probs, k_all, v_all, scratch,
):
    tokens = dec.shape[0]
    span = tokens + 2 * HALO
    for all_ref, own, i in ((k_all, keys, 0), (v_all, values, 1)):
        all_ref[0:HALO, :] = halo_lo[i]
        all_ref[HALO : HALO + tokens, :] = own[...]
        all_ref[HALO + tokens : span, :] = halo_hi[i]
    frame = lax.broadcasted_iota(jnp.int32, (span, tokens), 0)
    inside = (frame >= bounds[0:1, :]) & (frame < bounds[1:2, :])
    square = jnp.zeros((tokens, 1), F32)
    for h in range(HEADS):
        cols = slice(h * HD, (h + 1) * HD)
        x = dec[:, cols].astype(F32)
        query = query_of(x)[0].astype(BF)
        scores = mm(k_all[:, cols], query, NT) * INV_ROOT_HD
        weights = jnp.where(inside, jnp.exp(scores), 0.0)
        att = weights * (1.0 / jnp.sum(weights, axis=0, keepdims=True))
        probs[h] = att
        mixed = x + mm(att.astype(BF), v_all[:, cols], TN)
        hidden[:, cols] = mixed
        square = square + jnp.sum(mixed * mixed, axis=-1, keepdims=True)
    scale_h = lax.rsqrt(square * (1.0 / (HEADS * HD)) + NORM_EPS)
    table, is_first = slot_table(routes, 16)
    gate = slot_gates(table, is_first, gates)
    table = table.astype(BF)
    slots_to_travel(mm(table, (hidden[...] * scale_h).astype(BF)), scratch, 0)
    slots_to_travel(mm(table, cot[...]) * gate, scratch, 1)
    low = scratch[...].astype(BF)
    for d in range(sent.shape[0]):
        sent[d] = low


def rows_kernel(got, out, scratch):
    half = out.shape[0] // 2
    for kind in range(2):
        for j in range(got.shape[0]):
            start = kind * TRAVEL_ROWS
            scratch[j * TRAVEL_ROWS : (j + 1) * TRAVEL_ROWS, :] = got[
                j, start : start + TRAVEL_ROWS, :
            ].astype(F32)
        for c in range(16):
            out[kind * half : (kind + 1) * half, c * LANES : (c + 1) * LANES] = from_travel(
                scratch, half, c
            ).astype(BF)


def gelu_parts(pre_act):
    gauss_cdf = 0.5 * (1.0 + lax.erf(pre_act * ROOT_HALF))
    slope = gauss_cdf + pre_act * jnp.exp(-0.5 * pre_act * pre_act) * INV_ROOT_TWOPI
    return (pre_act * gauss_cdf, slope)


def send_halves(lhs, rhs_of, outs, scratches):
    half = lhs.shape[0] // 2
    for c in range(0, 16, 2):
        part = rhs_of(lhs, c)
        for i, scratch in enumerate(scratches):
            for k in range(2):
                scratch[pl.ds(c + k, half, stride=16), :] = part[
                    i * half : (i + 1) * half, k * LANES : (k + 1) * LANES
                ]
    for out, scratch in zip(outs, scratches):
        out[...] = scratch[...].astype(BF)


def expert_back_kernel(place, rows_own, rows_other, *refs):
    pieces, refs = refs[:-9], refs[-9:]
    own, other, gelu, up, down, sc_own, sc_other, rows_in, rows_grad = refs
    assemble(place, pieces, up, down)
    half = rows_own.shape[0] // 2
    for i, ref in enumerate((rows_own, rows_other)):
        rows_in[i * half : (i + 1) * half, :] = ref[0:half, :]
        rows_grad[i * half : (i + 1) * half, :] = ref[half : 2 * half, :]
    pre_act = mm(rows_in[...], up[...])
    value, slope = gelu_parts(pre_act)
    gelu[...] = value.astype(BF)
    grad_act = (mm(rows_grad[...], down[...], NT) * slope).astype(BF)
    send_halves(
        grad_act,
        lambda lhs, c: mm(lhs, up[c * LANES : (c + 2) * LANES, :], NT),
        (own, other),
        (sc_own, sc_other),
    )


def expert_out_kernel(gelu, down, own, other, sc_own, sc_other):
    send_halves(
        gelu[...],
        lambda lhs, c: mm(lhs, down[:, c * LANES : (c + 2) * LANES]),
        (own, other),
        (sc_own, sc_other),
    )


def assemble(place, pieces, up, down):
    x, zh = place[0], place[1]

    def put(part, block, x, zh):
        start = pl.multiple_of(((x & 3) * 4 + (zh & 3)) * LANES, LANES)
        if part == 0:
            up[pl.ds(start, LANES), :] = block[...]
        else:
            for q in range(4):
                cols = slice(q * LANES, (q + 1) * LANES)
                down[cols, pl.ds(start, LANES)] = block[:, cols]

    def put_ring(refs, first_zh):
        own, before, after, low, high = refs
        count = own.shape[0] // LANES
        for i in range(count):
            rows = pl.ds(i * LANES, LANES)
            for ref, step in ((own, 0), (before, 3), (after, 1)):
                put(i % 2, ref.at[rows], x + step, first_zh + i // 2)
            far, j = (low, i) if 2 * i < count else (high, i - count // 2)
            put(i % 2, far.at[pl.ds(j * LANES, LANES)], x + 2, first_zh + i // 2)

    put_ring(pieces[0:5], zh)
    put_ring(pieces[5:10], zh + 1)
    for i in range(4):
        for part in range(2):
            put(part, pieces[10].at[i, pl.ds(part * LANES, LANES)], i, zh + 3)


def slot_sum(back, scratch):
    total = back[0].astype(F32)
    for d in range(1, back.shape[0]):
        total = total + back[d].astype(F32)
    scratch[...] = total
    return jnp.concatenate([from_travel(scratch, SLOTS, c) for c in range(16)], axis=1)


def out_kernel(routes, gates, back, hidden, out, scratch):
    table, is_first = slot_table(routes)
    rows = slot_sum(back, scratch) * slot_gates(table, is_first, gates)
    out[...] = (hidden[...] + scatter_slots(table, rows)).astype(BF)


def attend_back_kernel(
    routes, back, cot, hidden, dec, probs, keys, values, halo_lo, halo_hi,
    grad_in, grad_k, grad_v, edge, send, k_all, v_all, scratch, grad_h,
):
    tokens = dec.shape[0]
    span = tokens + 2 * HALO
    for all_ref, own, i in ((k_all, keys, 0), (v_all, values, 1)):
        all_ref[0:HALO, :] = halo_lo[i]
        all_ref[HALO : HALO + tokens, :] = own[...]
        all_ref[HALO + tokens : span, :] = halo_hi[i]
    table, _ = slot_table(routes)
    grad_norm = scatter_slots(table, slot_sum(back, scratch))
    mixed = hidden[...]
    scale_h = lax.rsqrt(jnp.mean(mixed * mixed, axis=-1, keepdims=True) + NORM_EPS)
    normed = mixed * scale_h
    grad_h[...] = cot[...].astype(F32) + scale_h * (
        grad_norm - normed * jnp.mean(grad_norm * normed, axis=-1, keepdims=True)
    )
    for h in range(HEADS):
        cols = slice(h * HD, (h + 1) * HD)
        grad_hidden = grad_h[:, cols]
        grad_low = grad_hidden.astype(BF)
        att = probs[h]
        grad_probs = mm(v_all[:, cols], grad_low, NT)
        inner = jnp.sum(att * grad_probs, axis=0, keepdims=True)
        scores_low = (att * (grad_probs - inner) * INV_ROOT_HD).astype(BF)
        query, scale_q = query_of(dec[:, cols].astype(F32))
        grad_query = mm(scores_low, k_all[:, cols], TN)
        piece = scale_q * (
            grad_query - query * jnp.mean(grad_query * query, axis=-1, keepdims=True)
        )
        grad_in[:, cols] = (grad_hidden + piece).astype(BF)
        both = (
            mm(scores_low, query.astype(BF)),
            mm(att.astype(BF), grad_low),
        )
        for i, (grad, ref) in enumerate(zip(both, (grad_k, grad_v))):
            ref[:, cols] = grad[HALO : HALO + tokens, :].astype(BF)
            edge[i, 0, :, cols] = grad[HALO : 2 * HALO, :]
            edge[i, 1, :, cols] = grad[tokens : HALO + tokens, :]
            send[0, i, :, cols] = grad[0:HALO, :].astype(BF)
            send[1, i, :, cols] = grad[HALO + tokens : span, :].astype(BF)


def shift(value, axis, step):
    count = lax.axis_size(axis)
    return lax.ppermute(value, axis, [(i, (i + step) % count) for i in range(count)])


def neighbours(tail, head):
    axes = ("x", "zh", "y", "core")
    count = lax.axis_size(axes)
    return (
        lax.ppermute(tail, axes, [(i, i + 1) for i in range(count - 1)]),
        lax.ppermute(head, axes, [(i + 1, i) for i in range(count - 1)]),
    )


def exchange(sent):
    axes = ("dp", "zh", "y", "core")
    dp, zh, y, core = (lax.axis_size(axis) for axis in axes)
    groups = []
    for c in range(core):
        for run in range(zh):
            members = []
            for step in range(dp):
                z = (run * dp + step + 2 * c) % (dp * zh)
                members += [((z % dp * zh + z // dp) * y + i) * core + c for i in range(y)]
            groups.append(members)
    return lax.all_to_all(
        sent, axes, split_axis=0, concat_axis=0, axis_index_groups=groups, tiled=True
    )


def pack_weights(up_local, down_local):
    turned = down_local.reshape(4, LANES, LANES).transpose(1, 0, 2).reshape(LANES, 4 * LANES)
    return jnp.concatenate([up_local, turned], axis=0)


def ring_sides(block):
    return shift(block, "x", 1), shift(block, "x", -1)


def ring_opposite(before, after):
    half = before.shape[0] // 2
    return shift(before[:half], "x", 1), shift(after[half:], "x", -1)


def slot_rows(got):
    count = got.shape[0] * SLOT_LIMIT
    return call(
        rows_kernel,
        [shaped((2 * count, 16 * LANES), BF)],
        (got,),
        scratch=[pltpu.VMEM((count * 16, LANES), F32)],
    )[0]


def send_back(own, other):
    total = own.astype(F32) + shift(other, "core", 1).astype(F32)
    return exchange(total.astype(BF).reshape(16, TRAVEL_ROWS, LANES)).reshape(4, -1, LANES)


def shards(
    decoder_in, enc_keys, enc_values, win_start, win_end, routes, gate_probs, w_up, w_down, cotangent
):
    dec, keys, values, cot = decoder_in[0], enc_keys[0], enc_values[0], cotangent[0]
    tokens, feat = dec.shape
    span = tokens + 2 * HALO
    position = lax.axis_index(("x", "zh", "y", "core"))
    place = jnp.stack([lax.axis_index("x"), lax.axis_index("zh")]).astype(jnp.int32)
    bounds = jnp.stack([win_start[0], win_end[0]], axis=0) - (position * tokens - HALO)
    routes_t = routes[0].T
    gates_t = gate_probs[0].T

    packed = pack_weights(w_up[0], w_down[0])
    column = lax.all_gather(packed, "zh", axis=0, tiled=True)
    halo_lo, halo_hi = neighbours(
        jnp.stack([keys[tokens - HALO :], values[tokens - HALO :]]),
        jnp.stack([keys[:HALO], values[:HALO]]),
    )
    for_x, halo_lo, halo_hi = lax.optimization_barrier((packed, halo_lo, halo_hi))
    own_sides = ring_sides(for_x)
    own_opposite = ring_opposite(*own_sides)

    travel = (4, 2 * EXPERTS * TRAVEL_ROWS, LANES)
    sent, hidden, probs = call(
        attend_kernel,
        [shaped(travel, BF), shaped((tokens, feat), F32), shaped((HEADS, span, tokens), F32)],
        (routes_t, gates_t, bounds, dec, cot, keys, values, halo_lo, halo_hi),
        scratch=[
            pltpu.VMEM((span, feat), BF),
            pltpu.VMEM((span, feat), BF),
            pltpu.VMEM(travel[1:], F32),
        ],
    )
    sent, column, own_sides, own_opposite = lax.optimization_barrier(
        (sent, column, own_sides, own_opposite)
    )
    got = exchange(sent.reshape(16, 2 * TRAVEL_ROWS, LANES))
    block = packed.shape[0]
    nexts = [
        lax.dynamic_slice_in_dim(column, (place[1] + step) % 4 * block, block, 0)
        for step in range(1, 4)
    ]
    two, last = jnp.concatenate(nexts[:2], axis=0), nexts[2]
    last_x = lax.all_gather(last, "x", axis=0)
    two_sides = ring_sides(two)
    two_opposite = ring_opposite(*two_sides)
    got, two_sides = lax.optimization_barrier((got, two_sides))
    own_rows = slot_rows(got)
    other_rows = shift(own_rows, "core", 1)
    pieces = (packed, *own_sides, *own_opposite, two, *two_sides, *two_opposite, last_x)

    rows, units = own_rows.shape[0], 4 * LANES
    half = (rows // 2 * 16, LANES)
    back_own, back_other, gelu, up_full, down_full = call(
        expert_back_kernel,
        [
            shaped(half, BF),
            shaped(half, BF),
            shaped((rows, units), BF),
            shaped((feat, units), BF),
            shaped((units, feat), BF),
        ],
        (place, own_rows, other_rows, *pieces),
        scratch=[
            pltpu.VMEM(half, F32),
            pltpu.VMEM(half, F32),
            pltpu.VMEM((rows, feat), BF),
            pltpu.VMEM((rows, feat), BF),
        ],
        scalars=1,
    )
    back = send_back(back_own, back_other)
    value_own, value_other = call(
        expert_out_kernel,
        [shaped(half, BF), shaped(half, BF)],
        (gelu, down_full),
        scratch=[pltpu.VMEM(half, F32), pltpu.VMEM(half, F32)],
    )
    result = send_back(value_own, value_other)

    grad_in, grad_k, grad_v, edge, send = call(
        attend_back_kernel,
        [
            shaped((tokens, feat), BF),
            shaped((tokens, feat), BF),
            shaped((tokens, feat), BF),
            shaped((2, 2, HALO, feat), F32),
            shaped((2, 2, HALO, feat), BF),
        ],
        (routes_t, back, cot, hidden, dec, probs, keys, values, halo_lo, halo_hi),
        scratch=[
            pltpu.VMEM((span, feat), BF),
            pltpu.VMEM((span, feat), BF),
            pltpu.VMEM((SLOTS * 16, LANES), F32),
            pltpu.VMEM((tokens, feat), F32),
        ],
    )
    from_lo, from_hi = neighbours(send[1], send[0])
    (block_out,) = call(
        out_kernel,
        [shaped((tokens, feat), BF)],
        (routes_t, gates_t, result, hidden),
        scratch=[pltpu.VMEM((SLOTS * 16, LANES), F32)],
    )
    grads = []
    for i, grad in enumerate((grad_k, grad_v)):
        low = (edge[i, 0] + from_lo[i].astype(F32)).astype(BF)
        high = (edge[i, 1] + from_hi[i].astype(F32)).astype(BF)
        grad = lax.dynamic_update_slice(grad, low, (0, 0))
        grad = lax.dynamic_update_slice(grad, high, (tokens - HALO, 0))
        grads.append(grad)
    return (block_out[None], grad_in[None], grads[0][None], grads[1][None])


def solution(mesh):
    fine = Mesh(mesh.devices.reshape(4, 4, 4, 4, 2), ("dp", "x", "zh", "y", "core"))
    time = ("x", "zh", "y", "core")
    wide = P("dp", time, None)
    return jax.shard_map(
        shards,
        mesh=fine,
        in_specs=(
            wide,
            wide,
            wide,
            P("dp", time),
            P("dp", time),
            wide,
            wide,
            P(("y", "core"), ("x", "zh"), "dp"),
            P(("y", "core"), "dp", ("x", "zh")),
            wide,
        ),
        out_specs=(wide, wide, wide, wide),
        check_vma=False,
    )
```

```python
import math

import jax
import jax.numpy as jnp
from jax import lax
from jax.experimental import pallas as pl
from jax.experimental.pallas import tpu as pltpu
from jax.sharding import Mesh, PartitionSpec as P

HEADS = 16
HD = 128
HALO = 16
SLOT_LIMIT = 10
EXPERTS = 4
SLOTS = EXPERTS * SLOT_LIMIT
LANES = 128
TRAVEL_ROWS = SLOT_LIMIT * 16

NORM_EPS = 1e-06
ROOT_HALF = 1.0 / math.sqrt(2.0)
INV_ROOT_TWOPI = 1.0 / math.sqrt(2.0 * math.pi)
INV_ROOT_HD = 1.0 / math.sqrt(HD)

BF = jnp.bfloat16
F32 = jnp.float32
VMEM_LIMIT = 56 * 1024 * 1024

NT = (((1,), (1,)), ((), ()))
TN = (((0,), (0,)), ((), ()))


def mm(a, b, dims=(((1,), (0,)), ((), ()))):
    return lax.dot_general(a, b, dims, preferred_element_type=F32)


def call(body, outs, args, scratch=(), flops=10**8, scalars=0):
    nbytes = sum(math.prod(a.shape) * a.dtype.itemsize for a in args)
    nbytes += sum(math.prod(o.shape) * o.dtype.itemsize for o in outs)
    return pl.pallas_call(
        body,
        out_shape=outs,
        in_specs=[pl.BlockSpec(memory_space=pltpu.SMEM)] * scalars
        + [pl.BlockSpec(memory_space=pltpu.VMEM)] * (len(args) - scalars),
        out_specs=[pl.BlockSpec(memory_space=pltpu.VMEM)] * len(outs),
        scratch_shapes=list(scratch),
        compiler_params=pltpu.CompilerParams(vmem_limit_bytes=VMEM_LIMIT),
        cost_estimate=pl.CostEstimate(flops=flops, bytes_accessed=nbytes, transcendentals=0),
    )(*args)


def shaped(shape, dtype):
    return jax.ShapeDtypeStruct(shape, dtype)


def slot_table(routes_ref, stride=SLOT_LIMIT):
    tokens = routes_ref.shape[1]
    first, second = routes_ref[0:1, :], routes_ref[1:2, :]
    slot = lax.broadcasted_iota(jnp.int32, (EXPERTS * stride, tokens), 0)
    expert = jnp.zeros_like(slot)
    for e in range(1, EXPERTS):
        expert = expert + (slot >= e * stride).astype(jnp.int32)
    rank = (slot - expert * stride).astype(F32)
    is_first = first == expert
    member = is_first | (second == expert)
    before = lax.broadcasted_iota(jnp.int32, (tokens, tokens), 0)
    after = lax.broadcasted_iota(jnp.int32, (tokens, tokens), 1)
    earlier = mm(
        jnp.where(member, 1.0, 0.0).astype(BF), jnp.where(before < after, 1.0, 0.0).astype(BF)
    )
    table = jnp.where(member & (earlier == rank), 1.0, 0.0)
    return table, is_first


def slot_gates(table, is_first, gates_ref):
    gate = jnp.where(is_first, gates_ref[0:1, :], gates_ref[1:2, :])
    return jnp.sum(table * gate, axis=1, keepdims=True)


def from_travel(scratch, row_count, c, base=0):
    return scratch[pl.ds(base + c, row_count, stride=16), :]


def scatter_slots(table, rows):
    high = rows.astype(BF)
    low = (rows - high.astype(F32)).astype(BF)
    table_low = table.astype(BF)
    return mm(table_low, high, TN) + mm(table_low, low, TN)


def slots_to_travel(rows, scratch, kind):
    for e in range(EXPERTS):
        base = (2 * e + kind) * TRAVEL_ROWS
        for c in range(16):
            scratch[pl.ds(base + c, SLOT_LIMIT, stride=16), :] = rows[
                e * 16 : e * 16 + SLOT_LIMIT, c * LANES : (c + 1) * LANES
            ]


def query_of(x):
    scale = lax.rsqrt(jnp.mean(x * x, axis=-1, keepdims=True) + NORM_EPS)
    return x * scale, scale


def attend_kernel(
    routes, gates, bounds, dec, cot, keys, values, halo_lo, halo_hi,
    sent, hidden, probs, k_all, v_all, scratch,
):
    tokens = dec.shape[0]
    span = tokens + 2 * HALO
    for all_ref, own, i in ((k_all, keys, 0), (v_all, values, 1)):
        all_ref[0:HALO, :] = halo_lo[i]
        all_ref[HALO : HALO + tokens, :] = own[...]
        all_ref[HALO + tokens : span, :] = halo_hi[i]
    frame = lax.broadcasted_iota(jnp.int32, (span, tokens), 0)
    inside = (frame >= bounds[0:1, :]) & (frame < bounds[1:2, :])
    square = jnp.zeros((tokens, 1), F32)
    for h in range(HEADS):
        cols = slice(h * HD, (h + 1) * HD)
        x = dec[:, cols].astype(F32)
        query = query_of(x)[0].astype(BF)
        scores = mm(k_all[:, cols], query, NT) * INV_ROOT_HD
        weights = jnp.where(inside, jnp.exp(scores), 0.0)
        att = weights * (1.0 / jnp.sum(weights, axis=0, keepdims=True))
        probs[h] = att
        mixed = x + mm(att.astype(BF), v_all[:, cols], TN)
        hidden[:, cols] = mixed
        square = square + jnp.sum(mixed * mixed, axis=-1, keepdims=True)
    scale_h = lax.rsqrt(square * (1.0 / (HEADS * HD)) + NORM_EPS)
    table, is_first = slot_table(routes, 16)
    gate = slot_gates(table, is_first, gates)
    table = table.astype(BF)
    slots_to_travel(mm(table, (hidden[...] * scale_h).astype(BF)), scratch, 0)
    slots_to_travel(mm(table, cot[...]) * gate, scratch, 1)
    low = scratch[...].astype(BF)
    for d in range(sent.shape[0]):
        sent[d] = low


def rows_kernel(got, out):
    half, feat = out.shape[0] // 2, out.shape[1]
    for kind in range(2):
        rows = got[:, kind * TRAVEL_ROWS : (kind + 1) * TRAVEL_ROWS, :]
        out[kind * half : (kind + 1) * half, :] = rows.reshape(half, 16, LANES).reshape(half, feat)


def gelu_parts(pre_act):
    gauss_cdf = 0.5 * (1.0 + lax.erf(pre_act * ROOT_HALF))
    slope = gauss_cdf + pre_act * jnp.exp(-0.5 * pre_act * pre_act) * INV_ROOT_TWOPI
    return (pre_act * gauss_cdf, slope)


def send_halves(lhs, rhs_of, outs, scratch):
    half = lhs.shape[0] // 2
    for c in range(0, 16, 2):
        scratch[:, c * LANES : (c + 2) * LANES] = rhs_of(lhs, c).astype(BF)
    for i, out in enumerate(outs):
        out[...] = scratch[i * half : (i + 1) * half, :].reshape(out.shape)


def expert_back_kernel(place, rows_own, rows_other, *refs):
    pieces, refs = refs[:-8], refs[-8:]
    own, other, gelu, up, down, scratch, rows_in, rows_grad = refs
    assemble(place, pieces, up, down)
    half = rows_own.shape[0] // 2
    for i, ref in enumerate((rows_own, rows_other)):
        rows_in[i * half : (i + 1) * half, :] = ref[0:half, :]
        rows_grad[i * half : (i + 1) * half, :] = ref[half : 2 * half, :]
    pre_act = mm(rows_in[...], up[...])
    value, slope = gelu_parts(pre_act)
    gelu[...] = value.astype(BF)
    grad_act = (mm(rows_grad[...], down[...], NT) * slope).astype(BF)
    send_halves(
        grad_act,
        lambda lhs, c: mm(lhs, up[c * LANES : (c + 2) * LANES, :], NT),
        (own, other),
        scratch,
    )


def expert_out_kernel(gelu, down, own, other, scratch):
    send_halves(
        gelu[...],
        lambda lhs, c: mm(lhs, down[:, c * LANES : (c + 2) * LANES]),
        (own, other),
        scratch,
    )


def assemble(place, pieces, up, down):
    x, zh = place[0], place[1]

    def put(part, block, x, zh):
        start = pl.multiple_of(((x & 3) * 4 + (zh & 3)) * LANES, LANES)
        if part == 0:
            up[pl.ds(start, LANES), :] = block[...]
        else:
            for q in range(4):
                cols = slice(q * LANES, (q + 1) * LANES)
                down[cols, pl.ds(start, LANES)] = block[:, cols]

    def put_ring(refs, first_zh):
        own, before, after, low, high = refs
        count = own.shape[0] // LANES
        for i in range(count):
            rows = pl.ds(i * LANES, LANES)
            for ref, step in ((own, 0), (before, 3), (after, 1)):
                put(i % 2, ref.at[rows], x + step, first_zh + i // 2)
            far, j = (low, i) if 2 * i < count else (high, i - count // 2)
            put(i % 2, far.at[pl.ds(j * LANES, LANES)], x + 2, first_zh + i // 2)

    put_ring(pieces[0:5], zh)
    put_ring(pieces[5:10], zh + 1)
    for i in range(4):
        for part in range(2):
            put(part, pieces[10].at[i, pl.ds(part * LANES, LANES)], i, zh + 3)


def slot_sum(back, scratch):
    total = back[0].astype(F32)
    for d in range(1, back.shape[0]):
        total = total + back[d].astype(F32)
    scratch[...] = total
    return jnp.concatenate([from_travel(scratch, SLOTS, c) for c in range(16)], axis=1)


def out_kernel(routes, gates, back, hidden, out, scratch):
    table, is_first = slot_table(routes)
    rows = slot_sum(back, scratch) * slot_gates(table, is_first, gates)
    out[...] = (hidden[...] + scatter_slots(table, rows)).astype(BF)


def attend_back_kernel(
    routes, back, cot, hidden, dec, probs, keys, values, halo_lo, halo_hi,
    grad_in, grad_k, grad_v, edge, send_lo, send_hi, k_all, v_all, scratch, grad_h,
):
    tokens = dec.shape[0]
    span = tokens + 2 * HALO
    for all_ref, own, i in ((k_all, keys, 0), (v_all, values, 1)):
        all_ref[0:HALO, :] = halo_lo[i]
        all_ref[HALO : HALO + tokens, :] = own[...]
        all_ref[HALO + tokens : span, :] = halo_hi[i]
    table, _ = slot_table(routes)
    grad_norm = scatter_slots(table, slot_sum(back, scratch))
    mixed = hidden[...]
    scale_h = lax.rsqrt(jnp.mean(mixed * mixed, axis=-1, keepdims=True) + NORM_EPS)
    normed = mixed * scale_h
    grad_h[...] = cot[...].astype(F32) + scale_h * (
        grad_norm - normed * jnp.mean(grad_norm * normed, axis=-1, keepdims=True)
    )
    for h in range(HEADS):
        cols = slice(h * HD, (h + 1) * HD)
        grad_hidden = grad_h[:, cols]
        grad_low = grad_hidden.astype(BF)
        att = probs[h]
        grad_probs = mm(v_all[:, cols], grad_low, NT)
        inner = jnp.sum(att * grad_probs, axis=0, keepdims=True)
        scores_low = (att * (grad_probs - inner) * INV_ROOT_HD).astype(BF)
        query, scale_q = query_of(dec[:, cols].astype(F32))
        grad_query = mm(scores_low, k_all[:, cols], TN)
        piece = scale_q * (
            grad_query - query * jnp.mean(grad_query * query, axis=-1, keepdims=True)
        )
        grad_in[:, cols] = (grad_hidden + piece).astype(BF)
        both = (
            mm(scores_low, query.astype(BF)),
            mm(att.astype(BF), grad_low),
        )
        for i, (grad, ref) in enumerate(zip(both, (grad_k, grad_v))):
            ref[:, cols] = grad[HALO : HALO + tokens, :].astype(BF)
            edge[i, 0, :, cols] = grad[HALO : 2 * HALO, :]
            edge[i, 1, :, cols] = grad[tokens : HALO + tokens, :]
            send_lo[i, :, cols] = grad[0:HALO, :].astype(BF)
            send_hi[i, :, cols] = grad[HALO + tokens : span, :].astype(BF)


def shift(value, axis, step):
    count = lax.axis_size(axis)
    return lax.ppermute(value, axis, [(i, (i + step) % count) for i in range(count)])


def neighbours(tail, head):
    axes = ("x", "zh", "y", "core")
    count = lax.axis_size(axes)
    return (
        lax.ppermute(tail, axes, [(i, i + 1) for i in range(count - 1)]),
        lax.ppermute(head, axes, [(i + 1, i) for i in range(count - 1)]),
    )


def exchange(sent):
    axes = ("dp", "zh", "y", "core")
    dp, zh, y, core = (lax.axis_size(axis) for axis in axes)
    groups = []
    for c in range(core):
        for run in range(zh):
            members = []
            for step in range(dp):
                z = (run * dp + step + 2 * c) % (dp * zh)
                members += [((z % dp * zh + z // dp) * y + i) * core + c for i in range(y)]
            groups.append(members)
    return lax.all_to_all(
        sent, axes, split_axis=0, concat_axis=0, axis_index_groups=groups, tiled=True
    )


def pack_weights(up_local, down_local):
    turned = down_local.reshape(4, LANES, LANES).transpose(1, 0, 2).reshape(LANES, 4 * LANES)
    return jnp.concatenate([up_local, turned], axis=0)


def ring_sides(block):
    return shift(block, "x", 1), shift(block, "x", -1)


def ring_opposite(before, after):
    half = before.shape[0] // 2
    return shift(before[:half], "x", 1), shift(after[half:], "x", -1)


def slot_rows(got):
    count = got.shape[0] * SLOT_LIMIT
    return call(rows_kernel, [shaped((2 * count, 16 * LANES), BF)], (got,))[0]


def send_back(own, other):
    total = own + shift(other, "core", 1)
    return exchange(total.reshape(16, TRAVEL_ROWS, LANES)).reshape(4, -1, LANES)


def shards(
    decoder_in, enc_keys, enc_values, win_start, win_end, routes, gate_probs, w_up, w_down, cotangent
):
    dec, keys, values, cot = decoder_in[0], enc_keys[0], enc_values[0], cotangent[0]
    tokens, feat = dec.shape
    span = tokens + 2 * HALO
    position = lax.axis_index(("x", "zh", "y", "core"))
    place = jnp.stack([lax.axis_index("x"), lax.axis_index("zh")]).astype(jnp.int32)
    bounds = jnp.stack([win_start[0], win_end[0]], axis=0) - (position * tokens - HALO)
    routes_t = routes[0].T
    gates_t = gate_probs[0].T

    packed = pack_weights(w_up[0], w_down[0])
    column = lax.all_gather(packed, "zh", axis=0, tiled=True)
    halo_lo, halo_hi = neighbours(
        jnp.stack([keys[tokens - HALO :], values[tokens - HALO :]]),
        jnp.stack([keys[:HALO], values[:HALO]]),
    )
    for_x, halo_lo, halo_hi = lax.optimization_barrier((packed, halo_lo, halo_hi))
    own_sides = ring_sides(for_x)
    own_opposite = ring_opposite(*own_sides)

    travel = (4, 2 * EXPERTS * TRAVEL_ROWS, LANES)
    sent, hidden, probs = call(
        attend_kernel,
        [shaped(travel, BF), shaped((tokens, feat), F32), shaped((HEADS, span, tokens), F32)],
        (routes_t, gates_t, bounds, dec, cot, keys, values, halo_lo, halo_hi),
        scratch=[
            pltpu.VMEM((span, feat), BF),
            pltpu.VMEM((span, feat), BF),
            pltpu.VMEM(travel[1:], F32),
        ],
    )
    sent, column, own_sides, own_opposite = lax.optimization_barrier(
        (sent, column, own_sides, own_opposite)
    )
    got = exchange(sent.reshape(16, 2 * TRAVEL_ROWS, LANES))
    block = packed.shape[0]
    nexts = [
        lax.dynamic_slice_in_dim(column, (place[1] + step) % 4 * block, block, 0)
        for step in range(1, 4)
    ]
    two, last = jnp.concatenate(nexts[:2], axis=0), nexts[2]
    last_x = lax.all_gather(last, "x", axis=0)
    two_sides = ring_sides(two)
    two_opposite = ring_opposite(*two_sides)
    got, two_sides = lax.optimization_barrier((got, two_sides))
    own_rows = slot_rows(got)
    other_rows = shift(own_rows, "core", 1)
    pieces = (packed, *own_sides, *own_opposite, two, *two_sides, *two_opposite, last_x)

    rows, units = own_rows.shape[0], 4 * LANES
    half = (rows // 2, 16, LANES)
    back_own, back_other, gelu, up_full, down_full = call(
        expert_back_kernel,
        [
            shaped(half, BF),
            shaped(half, BF),
            shaped((rows, units), BF),
            shaped((feat, units), BF),
            shaped((units, feat), BF),
        ],
        (place, own_rows, other_rows, *pieces),
        scratch=[
            pltpu.VMEM((rows, feat), BF),
            pltpu.VMEM((rows, feat), BF),
            pltpu.VMEM((rows, feat), BF),
        ],
        scalars=1,
    )
    back = send_back(back_own, back_other)
    value_own, value_other = call(
        expert_out_kernel,
        [shaped(half, BF), shaped(half, BF)],
        (gelu, down_full),
        scratch=[pltpu.VMEM((rows, feat), BF)],
    )
    result = send_back(value_own, value_other)

    grad_in, grad_k, grad_v, edge, send_lo, send_hi = call(
        attend_back_kernel,
        [
            shaped((tokens, feat), BF),
            shaped((tokens, feat), BF),
            shaped((tokens, feat), BF),
            shaped((2, 2, HALO, feat), F32),
            shaped((2, HALO, feat), BF),
            shaped((2, HALO, feat), BF),
        ],
        (routes_t, back, cot, hidden, dec, probs, keys, values, halo_lo, halo_hi),
        scratch=[
            pltpu.VMEM((span, feat), BF),
            pltpu.VMEM((span, feat), BF),
            pltpu.VMEM((SLOTS * 16, LANES), F32),
            pltpu.VMEM((tokens, feat), F32),
        ],
    )
    from_lo, from_hi = neighbours(send_hi, send_lo)
    (block_out,) = call(
        out_kernel,
        [shaped((tokens, feat), BF)],
        (routes_t, gates_t, result, hidden),
        scratch=[pltpu.VMEM((SLOTS * 16, LANES), F32)],
    )
    grads = []
    for i, grad in enumerate((grad_k, grad_v)):
        low = (edge[i, 0] + from_lo[i].astype(F32)).astype(BF)
        high = (edge[i, 1] + from_hi[i].astype(F32)).astype(BF)
        grad = lax.dynamic_update_slice(grad, low, (0, 0))
        grad = lax.dynamic_update_slice(grad, high, (tokens - HALO, 0))
        grads.append(grad)
    return (block_out[None], grad_in[None], grads[0][None], grads[1][None])


def solution(mesh):
    fine = Mesh(mesh.devices.reshape(4, 4, 4, 4, 2), ("dp", "x", "zh", "y", "core"))
    time = ("x", "zh", "y", "core")
    wide = P("dp", time, None)
    return jax.shard_map(
        shards,
        mesh=fine,
        in_specs=(
            wide,
            wide,
            wide,
            P("dp", time),
            P("dp", time),
            wide,
            wide,
            P(("y", "core"), ("x", "zh"), "dp"),
            P(("y", "core"), "dp", ("x", "zh")),
            wide,
        ),
        out_specs=(wide, wide, wide, wide),
        check_vma=False,
    )
```

```python
import math

import jax
import jax.numpy as jnp
from jax import lax
from jax.experimental import pallas as pl
from jax.experimental.pallas import tpu as pltpu
from jax.sharding import Mesh, PartitionSpec as P

HEADS = 16
HD = 128
HALO = 16
SLOT_LIMIT = 10
EXPERTS = 4
SLOTS = EXPERTS * SLOT_LIMIT
LANES = 128
TRAVEL_ROWS = SLOT_LIMIT * 16

NORM_EPS = 1e-06
ROOT_HALF = 1.0 / math.sqrt(2.0)
INV_ROOT_TWOPI = 1.0 / math.sqrt(2.0 * math.pi)
INV_ROOT_HD = 1.0 / math.sqrt(HD)

BF = jnp.bfloat16
F32 = jnp.float32
VMEM_LIMIT = 56 * 1024 * 1024

NT = (((1,), (1,)), ((), ()))
TN = (((0,), (0,)), ((), ()))


def mm(a, b, dims=(((1,), (0,)), ((), ()))):
    return lax.dot_general(a, b, dims, preferred_element_type=F32)


def call(body, outs, args, scratch=(), flops=10**8, scalars=0):
    nbytes = sum(math.prod(a.shape) * a.dtype.itemsize for a in args)
    nbytes += sum(math.prod(o.shape) * o.dtype.itemsize for o in outs)
    return pl.pallas_call(
        body,
        out_shape=outs,
        in_specs=[pl.BlockSpec(memory_space=pltpu.SMEM)] * scalars
        + [pl.BlockSpec(memory_space=pltpu.VMEM)] * (len(args) - scalars),
        out_specs=[pl.BlockSpec(memory_space=pltpu.VMEM)] * len(outs),
        scratch_shapes=list(scratch),
        compiler_params=pltpu.CompilerParams(vmem_limit_bytes=VMEM_LIMIT),
        cost_estimate=pl.CostEstimate(flops=flops, bytes_accessed=nbytes, transcendentals=0),
    )(*args)


def shaped(shape, dtype):
    return jax.ShapeDtypeStruct(shape, dtype)


def slot_table(routes_ref, stride=SLOT_LIMIT):
    tokens = routes_ref.shape[1]
    first, second = routes_ref[0:1, :], routes_ref[1:2, :]
    slot = lax.broadcasted_iota(jnp.int32, (EXPERTS * stride, tokens), 0)
    expert = jnp.zeros_like(slot)
    for e in range(1, EXPERTS):
        expert = expert + (slot >= e * stride).astype(jnp.int32)
    rank = (slot - expert * stride).astype(F32)
    is_first = first == expert
    member = is_first | (second == expert)
    before = lax.broadcasted_iota(jnp.int32, (tokens, tokens), 0)
    after = lax.broadcasted_iota(jnp.int32, (tokens, tokens), 1)
    earlier = mm(
        jnp.where(member, 1.0, 0.0).astype(BF), jnp.where(before < after, 1.0, 0.0).astype(BF)
    )
    table = jnp.where(member & (earlier == rank), 1.0, 0.0)
    return table, is_first


def slot_gates(table, is_first, gates_ref):
    gate = jnp.where(is_first, gates_ref[0:1, :], gates_ref[1:2, :])
    return jnp.sum(table * gate, axis=1, keepdims=True)


def from_travel(scratch, row_count, c, base=0):
    return scratch[pl.ds(base + c, row_count, stride=16), :]


def scatter_slots(table, rows):
    high = rows.astype(BF)
    low = (rows - high.astype(F32)).astype(BF)
    table_low = table.astype(BF)
    return mm(table_low, high, TN) + mm(table_low, low, TN)


def slots_to_travel(rows, scratch, kind):
    for e in range(EXPERTS):
        base = (2 * e + kind) * TRAVEL_ROWS
        for c in range(16):
            scratch[pl.ds(base + c, SLOT_LIMIT, stride=16), :] = rows[
                e * 16 : e * 16 + SLOT_LIMIT, c * LANES : (c + 1) * LANES
            ]


def query_of(x):
    scale = lax.rsqrt(jnp.mean(x * x, axis=-1, keepdims=True) + NORM_EPS)
    return x * scale, scale


def attend_kernel(
    routes, gates, bounds, dec, cot, keys, values, halo_lo, halo_hi,
    sent, hidden, probs, k_all, v_all, scratch,
):
    tokens = dec.shape[0]
    span = tokens + 2 * HALO
    for all_ref, own, i in ((k_all, keys, 0), (v_all, values, 1)):
        all_ref[0:HALO, :] = halo_lo[i]
        all_ref[HALO : HALO + tokens, :] = own[...]
        all_ref[HALO + tokens : span, :] = halo_hi[i]
    frame = lax.broadcasted_iota(jnp.int32, (span, tokens), 0)
    inside = (frame >= bounds[0:1, :]) & (frame < bounds[1:2, :])
    square = jnp.zeros((tokens, 1), F32)
    for h in range(HEADS):
        cols = slice(h * HD, (h + 1) * HD)
        x = dec[:, cols].astype(F32)
        query = query_of(x)[0].astype(BF)
        scores = mm(k_all[:, cols], query, NT) * INV_ROOT_HD
        weights = jnp.where(inside, jnp.exp(scores), 0.0)
        att = weights * (1.0 / jnp.sum(weights, axis=0, keepdims=True))
        probs[h] = att
        mixed = x + mm(att.astype(BF), v_all[:, cols], TN)
        hidden[:, cols] = mixed
        square = square + jnp.sum(mixed * mixed, axis=-1, keepdims=True)
    scale_h = lax.rsqrt(square * (1.0 / (HEADS * HD)) + NORM_EPS)
    table, is_first = slot_table(routes, 16)
    gate = slot_gates(table, is_first, gates)
    table = table.astype(BF)
    slots_to_travel(mm(table, (hidden[...] * scale_h).astype(BF)), scratch, 0)
    slots_to_travel(mm(table, cot[...]) * gate, scratch, 1)
    low = scratch[...].astype(BF)
    for d in range(sent.shape[0]):
        sent[d] = low


def rows_kernel(got, out):
    half, feat = out.shape[0] // 2, out.shape[1]
    for kind in range(2):
        rows = got[:, kind * TRAVEL_ROWS : (kind + 1) * TRAVEL_ROWS, :]
        out[kind * half : (kind + 1) * half, :] = rows.reshape(half, 16, LANES).reshape(half, feat)


def gelu_parts(pre_act):
    gauss_cdf = 0.5 * (1.0 + lax.erf(pre_act * ROOT_HALF))
    slope = gauss_cdf + pre_act * jnp.exp(-0.5 * pre_act * pre_act) * INV_ROOT_TWOPI
    return (pre_act * gauss_cdf, slope)


def send_halves(lhs, rhs_of, outs, scratch):
    half = lhs.shape[0] // 2
    for c in range(0, 16, 2):
        scratch[:, c * LANES : (c + 2) * LANES] = rhs_of(lhs, c).astype(BF)
    for i, out in enumerate(outs):
        out[...] = scratch[i * half : (i + 1) * half, :].reshape(out.shape)


def expert_back_kernel(place, rows_own, rows_other, *refs):
    pieces, refs = refs[:-8], refs[-8:]
    own, other, gelu, up, down, scratch, rows_in, rows_grad = refs
    assemble(place, pieces, up, down)
    half = rows_own.shape[0] // 2
    for i, ref in enumerate((rows_own, rows_other)):
        rows_in[i * half : (i + 1) * half, :] = ref[0:half, :]
        rows_grad[i * half : (i + 1) * half, :] = ref[half : 2 * half, :]
    pre_act = mm(rows_in[...], up[...])
    value, slope = gelu_parts(pre_act)
    gelu[...] = value.astype(BF)
    grad_act = (mm(rows_grad[...], down[...], NT) * slope).astype(BF)
    send_halves(
        grad_act,
        lambda lhs, c: mm(lhs, up[c * LANES : (c + 2) * LANES, :], NT),
        (own, other),
        scratch,
    )


def expert_out_kernel(gelu, down, own, other, scratch):
    send_halves(
        gelu[...],
        lambda lhs, c: mm(lhs, down[:, c * LANES : (c + 2) * LANES]),
        (own, other),
        scratch,
    )


def assemble(place, pieces, up, down):
    column, before, after, low, high = pieces
    x, zh = place[0], place[1]

    def put(block, x, zh):
        start = pl.multiple_of(((x & 3) * 4 + (zh & 3)) * LANES, LANES)
        up[pl.ds(start, LANES), :] = block[0:LANES, :]
        for q in range(4):
            cols = slice(q * LANES, (q + 1) * LANES)
            down[cols, pl.ds(start, LANES)] = block[LANES : 2 * LANES, cols]

    for i, step_z in enumerate((0, 3, 1, 2)):
        rows = pl.ds(2 * LANES * i, 2 * LANES)
        for ref, step_x in ((column, 0), (before, 3), (after, 1)):
            put(ref.at[rows], x + step_x, zh + step_z)
        far = (low, high)[i // 2]
        put(far.at[pl.ds(2 * LANES * (i % 2), 2 * LANES)], x + 2, zh + step_z)


def slot_sum(back, scratch):
    total = back[0].astype(F32)
    for d in range(1, back.shape[0]):
        total = total + back[d].astype(F32)
    scratch[...] = total
    return jnp.concatenate([from_travel(scratch, SLOTS, c) for c in range(16)], axis=1)


def out_kernel(routes, gates, back, hidden, out, scratch):
    table, is_first = slot_table(routes)
    rows = slot_sum(back, scratch) * slot_gates(table, is_first, gates)
    out[...] = (hidden[...] + scatter_slots(table, rows)).astype(BF)


def attend_back_kernel(
    routes, back, cot, hidden, dec, probs, keys, values, halo_lo, halo_hi,
    grad_in, grad_k, grad_v, edge, send_lo, send_hi, k_all, v_all, scratch, grad_h,
):
    tokens = dec.shape[0]
    span = tokens + 2 * HALO
    for all_ref, own, i in ((k_all, keys, 0), (v_all, values, 1)):
        all_ref[0:HALO, :] = halo_lo[i]
        all_ref[HALO : HALO + tokens, :] = own[...]
        all_ref[HALO + tokens : span, :] = halo_hi[i]
    table, _ = slot_table(routes)
    grad_norm = scatter_slots(table, slot_sum(back, scratch))
    mixed = hidden[...]
    scale_h = lax.rsqrt(jnp.mean(mixed * mixed, axis=-1, keepdims=True) + NORM_EPS)
    normed = mixed * scale_h
    grad_h[...] = cot[...].astype(F32) + scale_h * (
        grad_norm - normed * jnp.mean(grad_norm * normed, axis=-1, keepdims=True)
    )
    for h in range(HEADS):
        cols = slice(h * HD, (h + 1) * HD)
        grad_hidden = grad_h[:, cols]
        grad_low = grad_hidden.astype(BF)
        att = probs[h]
        grad_probs = mm(v_all[:, cols], grad_low, NT)
        inner = jnp.sum(att * grad_probs, axis=0, keepdims=True)
        scores_low = (att * (grad_probs - inner) * INV_ROOT_HD).astype(BF)
        query, scale_q = query_of(dec[:, cols].astype(F32))
        grad_query = mm(scores_low, k_all[:, cols], TN)
        piece = scale_q * (
            grad_query - query * jnp.mean(grad_query * query, axis=-1, keepdims=True)
        )
        grad_in[:, cols] = (grad_hidden + piece).astype(BF)
        both = (
            mm(scores_low, query.astype(BF)),
            mm(att.astype(BF), grad_low),
        )
        for i, (grad, ref) in enumerate(zip(both, (grad_k, grad_v))):
            ref[:, cols] = grad[HALO : HALO + tokens, :].astype(BF)
            edge[i, 0, :, cols] = grad[HALO : 2 * HALO, :]
            edge[i, 1, :, cols] = grad[tokens : HALO + tokens, :]
            send_lo[i, :, cols] = grad[0:HALO, :].astype(BF)
            send_hi[i, :, cols] = grad[HALO + tokens : span, :].astype(BF)


def shift(value, axis, step):
    count = lax.axis_size(axis)
    return lax.ppermute(value, axis, [(i, (i + step) % count) for i in range(count)])


def neighbours(tail, head):
    axes = ("x", "zh", "y", "core")
    count = lax.axis_size(axes)
    return (
        lax.ppermute(tail, axes, [(i, i + 1) for i in range(count - 1)]),
        lax.ppermute(head, axes, [(i + 1, i) for i in range(count - 1)]),
    )


def exchange(sent):
    axes = ("dp", "zh", "y", "core")
    dp, zh, y, core = (lax.axis_size(axis) for axis in axes)
    groups = []
    for c in range(core):
        for run in range(zh):
            members = []
            for step in range(dp):
                z = (run * dp + step + 2 * c) % (dp * zh)
                members += [((z % dp * zh + z // dp) * y + i) * core + c for i in range(y)]
            groups.append(members)
    return lax.all_to_all(
        sent, axes, split_axis=0, concat_axis=0, axis_index_groups=groups, tiled=True
    )


def pack_weights(up_local, down_local):
    turned = down_local.reshape(4, LANES, LANES).transpose(1, 0, 2).reshape(LANES, 4 * LANES)
    return jnp.concatenate([up_local, turned], axis=0)


def ring_sides(block, axis):
    return shift(block, axis, 1), shift(block, axis, -1)


def ring_opposite(before, after, axis):
    half = before.shape[0] // 2
    return shift(before[:half], axis, 1), shift(after[half:], axis, -1)


def slot_rows(got):
    count = got.shape[0] * SLOT_LIMIT
    return call(rows_kernel, [shaped((2 * count, 16 * LANES), BF)], (got,))[0]


def send_back(own, other):
    total = own + shift(other, "core", 1)
    return exchange(total.reshape(16, TRAVEL_ROWS, LANES)).reshape(4, -1, LANES)


def shards(
    decoder_in, enc_keys, enc_values, win_start, win_end, routes, gate_probs, w_up, w_down, cotangent
):
    dec, keys, values, cot = decoder_in[0], enc_keys[0], enc_values[0], cotangent[0]
    tokens, feat = dec.shape
    span = tokens + 2 * HALO
    position = lax.axis_index(("x", "zh", "y", "core"))
    place = jnp.stack([lax.axis_index("x"), lax.axis_index("zh")]).astype(jnp.int32)
    bounds = jnp.stack([win_start[0], win_end[0]], axis=0) - (position * tokens - HALO)
    routes_t = routes[0].T
    gates_t = gate_probs[0].T

    packed = pack_weights(w_up[0], w_down[0])
    sides_z = ring_sides(packed, "zh")
    far = ring_opposite(*sides_z, "zh")
    halo_lo, halo_hi = neighbours(
        jnp.stack([keys[tokens - HALO :], values[tokens - HALO :]]),
        jnp.stack([keys[:HALO], values[:HALO]]),
    )
    dec, sides_z = lax.optimization_barrier((dec, sides_z))

    travel = (4, 2 * EXPERTS * TRAVEL_ROWS, LANES)
    sent, hidden, probs = call(
        attend_kernel,
        [shaped(travel, BF), shaped((tokens, feat), F32), shaped((HEADS, span, tokens), F32)],
        (routes_t, gates_t, bounds, dec, cot, keys, values, halo_lo, halo_hi),
        scratch=[
            pltpu.VMEM((span, feat), BF),
            pltpu.VMEM((span, feat), BF),
            pltpu.VMEM(travel[1:], F32),
        ],
    )
    sent, far = lax.optimization_barrier((sent, far))
    got = exchange(sent.reshape(16, 2 * TRAVEL_ROWS, LANES))
    column = jnp.concatenate([packed, *sides_z, *far], axis=0)
    sides_x = ring_sides(column, "x")
    got, sides_x = lax.optimization_barrier((got, sides_x))
    own_rows = slot_rows(got)
    other_rows = shift(own_rows, "core", 1)
    pieces = (column, *sides_x, *ring_opposite(*sides_x, "x"))

    rows, units = own_rows.shape[0], 4 * LANES
    half = (rows // 2, 16, LANES)
    back_own, back_other, gelu, up_full, down_full = call(
        expert_back_kernel,
        [
            shaped(half, BF),
            shaped(half, BF),
            shaped((rows, units), BF),
            shaped((feat, units), BF),
            shaped((units, feat), BF),
        ],
        (place, own_rows, other_rows, *pieces),
        scratch=[
            pltpu.VMEM((rows, feat), BF),
            pltpu.VMEM((rows, feat), BF),
            pltpu.VMEM((rows, feat), BF),
        ],
        scalars=1,
    )
    back = send_back(back_own, back_other)
    value_own, value_other = call(
        expert_out_kernel,
        [shaped(half, BF), shaped(half, BF)],
        (gelu, down_full),
        scratch=[pltpu.VMEM((rows, feat), BF)],
    )
    result = send_back(value_own, value_other)

    grad_in, grad_k, grad_v, edge, send_lo, send_hi = call(
        attend_back_kernel,
        [
            shaped((tokens, feat), BF),
            shaped((tokens, feat), BF),
            shaped((tokens, feat), BF),
            shaped((2, 2, HALO, feat), F32),
            shaped((2, HALO, feat), BF),
            shaped((2, HALO, feat), BF),
        ],
        (routes_t, back, cot, hidden, dec, probs, keys, values, halo_lo, halo_hi),
        scratch=[
            pltpu.VMEM((span, feat), BF),
            pltpu.VMEM((span, feat), BF),
            pltpu.VMEM((SLOTS * 16, LANES), F32),
            pltpu.VMEM((tokens, feat), F32),
        ],
    )
    from_lo, from_hi = neighbours(send_hi, send_lo)
    (block_out,) = call(
        out_kernel,
        [shaped((tokens, feat), BF)],
        (routes_t, gates_t, result, hidden),
        scratch=[pltpu.VMEM((SLOTS * 16, LANES), F32)],
    )
    grads = []
    for i, grad in enumerate((grad_k, grad_v)):
        low = (edge[i, 0] + from_lo[i].astype(F32)).astype(BF)
        high = (edge[i, 1] + from_hi[i].astype(F32)).astype(BF)
        grad = lax.dynamic_update_slice(grad, low, (0, 0))
        grad = lax.dynamic_update_slice(grad, high, (tokens - HALO, 0))
        grads.append(grad)
    return (block_out[None], grad_in[None], grads[0][None], grads[1][None])


def solution(mesh):
    fine = Mesh(mesh.devices.reshape(4, 4, 4, 4, 2), ("dp", "x", "zh", "y", "core"))
    time = ("x", "zh", "y", "core")
    wide = P("dp", time, None)
    return jax.shard_map(
        shards,
        mesh=fine,
        in_specs=(
            wide,
            wide,
            wide,
            P("dp", time),
            P("dp", time),
            wide,
            wide,
            P(("y", "core"), ("x", "zh"), "dp"),
            P(("y", "core"), "dp", ("x", "zh")),
            wide,
        ),
        out_specs=(wide, wide, wide, wide),
        check_vma=False,
    )
```

```python
import math

import jax
import jax.numpy as jnp
from jax import lax
from jax.experimental import pallas as pl
from jax.experimental.pallas import tpu as pltpu
from jax.sharding import Mesh, PartitionSpec as P

HEADS = 16
HD = 128
HALO = 16
SLOT_LIMIT = 10
EXPERTS = 4
SLOTS = EXPERTS * SLOT_LIMIT
LANES = 128
TRAVEL_ROWS = SLOT_LIMIT * 16

NORM_EPS = 1e-06
ROOT_HALF = 1.0 / math.sqrt(2.0)
INV_ROOT_TWOPI = 1.0 / math.sqrt(2.0 * math.pi)
INV_ROOT_HD = 1.0 / math.sqrt(HD)

BF = jnp.bfloat16
F32 = jnp.float32
VMEM_LIMIT = 56 * 1024 * 1024

NT = (((1,), (1,)), ((), ()))
TN = (((0,), (0,)), ((), ()))


def mm(a, b, dims=(((1,), (0,)), ((), ()))):
    return lax.dot_general(a, b, dims, preferred_element_type=F32)


def call(body, outs, args, scratch=(), flops=10**8, scalars=0):
    nbytes = sum(math.prod(a.shape) * a.dtype.itemsize for a in args)
    nbytes += sum(math.prod(o.shape) * o.dtype.itemsize for o in outs)
    return pl.pallas_call(
        body,
        out_shape=outs,
        in_specs=[pl.BlockSpec(memory_space=pltpu.SMEM)] * scalars
        + [pl.BlockSpec(memory_space=pltpu.VMEM)] * (len(args) - scalars),
        out_specs=[pl.BlockSpec(memory_space=pltpu.VMEM)] * len(outs),
        scratch_shapes=list(scratch),
        compiler_params=pltpu.CompilerParams(vmem_limit_bytes=VMEM_LIMIT),
        cost_estimate=pl.CostEstimate(flops=flops, bytes_accessed=nbytes, transcendentals=0),
    )(*args)


def shaped(shape, dtype):
    return jax.ShapeDtypeStruct(shape, dtype)


def slot_table(routes_ref, stride=SLOT_LIMIT):
    tokens = routes_ref.shape[1]
    first, second = routes_ref[0:1, :], routes_ref[1:2, :]
    slot = lax.broadcasted_iota(jnp.int32, (EXPERTS * stride, tokens), 0)
    expert = jnp.zeros_like(slot)
    for e in range(1, EXPERTS):
        expert = expert + (slot >= e * stride).astype(jnp.int32)
    rank = (slot - expert * stride).astype(F32)
    is_first = first == expert
    member = is_first | (second == expert)
    before = lax.broadcasted_iota(jnp.int32, (tokens, tokens), 0)
    after = lax.broadcasted_iota(jnp.int32, (tokens, tokens), 1)
    earlier = mm(
        jnp.where(member, 1.0, 0.0).astype(BF), jnp.where(before < after, 1.0, 0.0).astype(BF)
    )
    table = jnp.where(member & (earlier == rank), 1.0, 0.0)
    return table, is_first


def slot_gates(table, is_first, gates_ref):
    gate = jnp.where(is_first, gates_ref[0:1, :], gates_ref[1:2, :])
    return jnp.sum(table * gate, axis=1, keepdims=True)


def from_travel(scratch, row_count, c, base=0):
    return scratch[pl.ds(base + c, row_count, stride=16), :]


def scatter_slots(table, rows):
    high = rows.astype(BF)
    low = (rows - high.astype(F32)).astype(BF)
    table_low = table.astype(BF)
    return mm(table_low, high, TN) + mm(table_low, low, TN)


def slots_to_travel(rows, scratch, kind):
    for e in range(EXPERTS):
        base = (2 * e + kind) * TRAVEL_ROWS
        for c in range(16):
            scratch[pl.ds(base + c, SLOT_LIMIT, stride=16), :] = rows[
                e * 16 : e * 16 + SLOT_LIMIT, c * LANES : (c + 1) * LANES
            ]


def query_of(x):
    scale = lax.rsqrt(jnp.mean(x * x, axis=-1, keepdims=True) + NORM_EPS)
    return x * scale, scale


def attend_kernel(
    routes, gates, bounds, dec, cot, keys, values, halo_lo, halo_hi,
    sent, hidden, probs, k_all, v_all, scratch,
):
    tokens = dec.shape[0]
    span = tokens + 2 * HALO
    for all_ref, own, i in ((k_all, keys, 0), (v_all, values, 1)):
        all_ref[0:HALO, :] = halo_lo[i]
        all_ref[HALO : HALO + tokens, :] = own[...]
        all_ref[HALO + tokens : span, :] = halo_hi[i]
    frame = lax.broadcasted_iota(jnp.int32, (span, tokens), 0)
    inside = (frame >= bounds[0:1, :]) & (frame < bounds[1:2, :])
    square = jnp.zeros((tokens, 1), F32)
    for h in range(HEADS):
        cols = slice(h * HD, (h + 1) * HD)
        x = dec[:, cols].astype(F32)
        query = query_of(x)[0].astype(BF)
        scores = mm(k_all[:, cols], query, NT) * INV_ROOT_HD
        weights = jnp.where(inside, jnp.exp(scores), 0.0)
        att = weights * (1.0 / jnp.sum(weights, axis=0, keepdims=True))
        probs[h] = att
        mixed = x + mm(att.astype(BF), v_all[:, cols], TN)
        hidden[:, cols] = mixed
        square = square + jnp.sum(mixed * mixed, axis=-1, keepdims=True)
    scale_h = lax.rsqrt(square * (1.0 / (HEADS * HD)) + NORM_EPS)
    table, is_first = slot_table(routes, 16)
    gate = slot_gates(table, is_first, gates)
    table = table.astype(BF)
    slots_to_travel(mm(table, (hidden[...] * scale_h).astype(BF)), scratch, 0)
    slots_to_travel(mm(table, cot[...]) * gate, scratch, 1)
    low = scratch[...].astype(BF)
    for d in range(sent.shape[0]):
        sent[d] = low


def rows_kernel(got, out):
    half, feat = out.shape[0] // 2, out.shape[1]
    for kind in range(2):
        rows = got[:, kind * TRAVEL_ROWS : (kind + 1) * TRAVEL_ROWS, :]
        out[kind * half : (kind + 1) * half, :] = rows.reshape(half, 16, LANES).reshape(half, feat)


def gelu_parts(pre_act):
    gauss_cdf = 0.5 * (1.0 + lax.erf(pre_act * ROOT_HALF))
    slope = gauss_cdf + pre_act * jnp.exp(-0.5 * pre_act * pre_act) * INV_ROOT_TWOPI
    return (pre_act * gauss_cdf, slope)


def send_halves(lhs, rhs_of, outs, scratch):
    half = lhs.shape[0] // 2
    for c in range(0, 16, 2):
        scratch[:, c * LANES : (c + 2) * LANES] = rhs_of(lhs, c).astype(BF)
    for i, out in enumerate(outs):
        out[...] = scratch[i * half : (i + 1) * half, :].reshape(out.shape)


def expert_back_kernel(place, rows_own, rows_other, *refs):
    pieces, refs = refs[:-8], refs[-8:]
    own, other, gelu, up, down, scratch, rows_in, rows_grad = refs
    assemble(place, pieces, up, down)
    half = rows_own.shape[0] // 2
    for i, ref in enumerate((rows_own, rows_other)):
        rows_in[i * half : (i + 1) * half, :] = ref[0:half, :]
        rows_grad[i * half : (i + 1) * half, :] = ref[half : 2 * half, :]
    pre_act = mm(rows_in[...], up[...])
    value, slope = gelu_parts(pre_act)
    gelu[...] = value.astype(BF)
    grad_act = (mm(rows_grad[...], down[...], NT) * slope).astype(BF)
    send_halves(
        grad_act,
        lambda lhs, c: mm(lhs, up[c * LANES : (c + 2) * LANES, :], NT),
        (own, other),
        scratch,
    )


def expert_out_kernel(gelu, down, own, other, scratch):
    send_halves(
        gelu[...],
        lambda lhs, c: mm(lhs, down[:, c * LANES : (c + 2) * LANES]),
        (own, other),
        scratch,
    )


def assemble(place, pieces, up, down):
    column, before, after, low, high = pieces
    x, zh = place[0], place[1]

    def put(block, x, zh):
        start = pl.multiple_of(((x & 3) * 4 + (zh & 3)) * LANES, LANES)
        up[pl.ds(start, LANES), :] = block[0:LANES, :]
        for q in range(4):
            cols = slice(q * LANES, (q + 1) * LANES)
            down[cols, pl.ds(start, LANES)] = block[LANES : 2 * LANES, cols]

    for i, step_z in enumerate((0, 3, 1, 2)):
        rows = pl.ds(2 * LANES * i, 2 * LANES)
        for ref, step_x in ((column, 0), (before, 3), (after, 1)):
            put(ref.at[rows], x + step_x, zh + step_z)
        far = (low, high)[i // 2]
        put(far.at[pl.ds(2 * LANES * (i % 2), 2 * LANES)], x + 2, zh + step_z)


def slot_sum(back, scratch):
    total = back[0].astype(F32)
    for d in range(1, back.shape[0]):
        total = total + back[d].astype(F32)
    scratch[...] = total
    return jnp.concatenate([from_travel(scratch, SLOTS, c) for c in range(16)], axis=1)


def out_kernel(routes, gates, back, hidden, out, scratch):
    table, is_first = slot_table(routes)
    rows = slot_sum(back, scratch) * slot_gates(table, is_first, gates)
    out[...] = (hidden[...] + scatter_slots(table, rows)).astype(BF)


def attend_back_kernel(
    routes, back, cot, hidden, dec, probs, keys, values, halo_lo, halo_hi,
    grad_in, grad_k, grad_v, edge, send_lo, send_hi, k_all, v_all, scratch, grad_h,
):
    tokens = dec.shape[0]
    span = tokens + 2 * HALO
    for all_ref, own, i in ((k_all, keys, 0), (v_all, values, 1)):
        all_ref[0:HALO, :] = halo_lo[i]
        all_ref[HALO : HALO + tokens, :] = own[...]
        all_ref[HALO + tokens : span, :] = halo_hi[i]
    table, _ = slot_table(routes)
    grad_norm = scatter_slots(table, slot_sum(back, scratch))
    mixed = hidden[...]
    scale_h = lax.rsqrt(jnp.mean(mixed * mixed, axis=-1, keepdims=True) + NORM_EPS)
    normed = mixed * scale_h
    grad_h[...] = cot[...].astype(F32) + scale_h * (
        grad_norm - normed * jnp.mean(grad_norm * normed, axis=-1, keepdims=True)
    )
    for h in range(HEADS):
        cols = slice(h * HD, (h + 1) * HD)
        grad_hidden = grad_h[:, cols]
        grad_low = grad_hidden.astype(BF)
        att = probs[h]
        grad_probs = mm(v_all[:, cols], grad_low, NT)
        inner = jnp.sum(att * grad_probs, axis=0, keepdims=True)
        scores_low = (att * (grad_probs - inner) * INV_ROOT_HD).astype(BF)
        query, scale_q = query_of(dec[:, cols].astype(F32))
        grad_query = mm(scores_low, k_all[:, cols], TN)
        piece = scale_q * (
            grad_query - query * jnp.mean(grad_query * query, axis=-1, keepdims=True)
        )
        grad_in[:, cols] = (grad_hidden + piece).astype(BF)
        both = (
            mm(scores_low, query.astype(BF)),
            mm(att.astype(BF), grad_low),
        )
        for i, (grad, ref) in enumerate(zip(both, (grad_k, grad_v))):
            ref[:, cols] = grad[HALO : HALO + tokens, :].astype(BF)
            edge[i, 0, :, cols] = grad[HALO : 2 * HALO, :]
            edge[i, 1, :, cols] = grad[tokens : HALO + tokens, :]
            send_lo[i, :, cols] = grad[0:HALO, :].astype(BF)
            send_hi[i, :, cols] = grad[HALO + tokens : span, :].astype(BF)


def shift(value, axis, step):
    count = lax.axis_size(axis)
    return lax.ppermute(value, axis, [(i, (i + step) % count) for i in range(count)])


def neighbours(tail, head):
    axes = ("x", "zh", "y", "core")
    count = lax.axis_size(axes)
    return (
        lax.ppermute(tail, axes, [(i, i + 1) for i in range(count - 1)]),
        lax.ppermute(head, axes, [(i + 1, i) for i in range(count - 1)]),
    )


def exchange(sent):
    axes = ("dp", "zh", "y", "core")
    dp, zh, y, core = (lax.axis_size(axis) for axis in axes)
    groups = []
    for c in range(core):
        for run in range(zh):
            members = []
            for step in range(dp):
                z = (run * dp + step + 2 * c) % (dp * zh)
                members += [((z % dp * zh + z // dp) * y + i) * core + c for i in range(y)]
            groups.append(members)
    return lax.all_to_all(
        sent, axes, split_axis=0, concat_axis=0, axis_index_groups=groups, tiled=True
    )


def pack_weights(up_local, down_local):
    turned = down_local.reshape(4, LANES, LANES).transpose(1, 0, 2).reshape(LANES, 4 * LANES)
    return jnp.concatenate([up_local, turned], axis=0)


def ring_sides(block, axis):
    return shift(block, axis, 1), shift(block, axis, -1)


def ring_opposite(before, after, axis):
    half = before.shape[0] // 2
    return shift(before[:half], axis, 1), shift(after[half:], axis, -1)


def slot_rows(got):
    count = got.shape[0] * SLOT_LIMIT
    return call(rows_kernel, [shaped((2 * count, 16 * LANES), BF)], (got,))[0]


def send_back(own, other):
    total = own + shift(other, "core", 1)
    return exchange(total.reshape(16, TRAVEL_ROWS, LANES)).reshape(4, -1, LANES)


def shards(
    decoder_in, enc_keys, enc_values, win_start, win_end, routes, gate_probs, w_up, w_down, cotangent
):
    dec, keys, values, cot = decoder_in[0], enc_keys[0], enc_values[0], cotangent[0]
    tokens, feat = dec.shape
    span = tokens + 2 * HALO
    position = lax.axis_index(("x", "zh", "y", "core"))
    place = jnp.stack([lax.axis_index("x"), lax.axis_index("zh")]).astype(jnp.int32)
    bounds = jnp.stack([win_start[0], win_end[0]], axis=0) - (position * tokens - HALO)
    routes_t = routes[0].T
    gates_t = gate_probs[0].T

    packed = pack_weights(w_up[0], w_down[0])
    sides_z = ring_sides(packed, "zh")
    far = ring_opposite(*sides_z, "zh")
    halo_lo, halo_hi = neighbours(
        jnp.stack([keys[tokens - HALO :], values[tokens - HALO :]]),
        jnp.stack([keys[:HALO], values[:HALO]]),
    )
    dec, sides_z = lax.optimization_barrier((dec, sides_z))

    travel = (4, 2 * EXPERTS * TRAVEL_ROWS, LANES)
    sent, hidden, probs = call(
        attend_kernel,
        [shaped(travel, BF), shaped((tokens, feat), F32), shaped((HEADS, span, tokens), F32)],
        (routes_t, gates_t, bounds, dec, cot, keys, values, halo_lo, halo_hi),
        scratch=[
            pltpu.VMEM((span, feat), BF),
            pltpu.VMEM((span, feat), BF),
            pltpu.VMEM(travel[1:], F32),
        ],
    )
    sent, far = lax.optimization_barrier((sent, far))
    got = exchange(sent.reshape(16, 2 * TRAVEL_ROWS, LANES))
    column = jnp.concatenate([packed, *sides_z, *far], axis=0)
    sides_x = ring_sides(column, "x")
    got, sides_x = lax.optimization_barrier((got, sides_x))
    own_rows = slot_rows(got)
    opposite = ring_opposite(*sides_x, "x")
    to_swap, opposite = lax.optimization_barrier((own_rows, opposite))
    other_rows = shift(to_swap, "core", 1)
    pieces = (column, *sides_x, *opposite)

    rows, units = own_rows.shape[0], 4 * LANES
    half = (rows // 2, 16, LANES)
    back_own, back_other, gelu, up_full, down_full = call(
        expert_back_kernel,
        [
            shaped(half, BF),
            shaped(half, BF),
            shaped((rows, units), BF),
            shaped((feat, units), BF),
            shaped((units, feat), BF),
        ],
        (place, own_rows, other_rows, *pieces),
        scratch=[
            pltpu.VMEM((rows, feat), BF),
            pltpu.VMEM((rows, feat), BF),
            pltpu.VMEM((rows, feat), BF),
        ],
        scalars=1,
    )
    back = send_back(back_own, back_other)
    value_own, value_other = call(
        expert_out_kernel,
        [shaped(half, BF), shaped(half, BF)],
        (gelu, down_full),
        scratch=[pltpu.VMEM((rows, feat), BF)],
    )
    result = send_back(value_own, value_other)

    grad_in, grad_k, grad_v, edge, send_lo, send_hi = call(
        attend_back_kernel,
        [
            shaped((tokens, feat), BF),
            shaped((tokens, feat), BF),
            shaped((tokens, feat), BF),
            shaped((2, 2, HALO, feat), F32),
            shaped((2, HALO, feat), BF),
            shaped((2, HALO, feat), BF),
        ],
        (routes_t, back, cot, hidden, dec, probs, keys, values, halo_lo, halo_hi),
        scratch=[
            pltpu.VMEM((span, feat), BF),
            pltpu.VMEM((span, feat), BF),
            pltpu.VMEM((SLOTS * 16, LANES), F32),
            pltpu.VMEM((tokens, feat), F32),
        ],
    )
    from_lo, from_hi = neighbours(send_hi, send_lo)
    (block_out,) = call(
        out_kernel,
        [shaped((tokens, feat), BF)],
        (routes_t, gates_t, result, hidden),
        scratch=[pltpu.VMEM((SLOTS * 16, LANES), F32)],
    )
    grads = []
    for i, grad in enumerate((grad_k, grad_v)):
        low = (edge[i, 0] + from_lo[i].astype(F32)).astype(BF)
        high = (edge[i, 1] + from_hi[i].astype(F32)).astype(BF)
        grad = lax.dynamic_update_slice(grad, low, (0, 0))
        grad = lax.dynamic_update_slice(grad, high, (tokens - HALO, 0))
        grads.append(grad)
    return (block_out[None], grad_in[None], grads[0][None], grads[1][None])


def solution(mesh):
    fine = Mesh(mesh.devices.reshape(4, 4, 4, 4, 2), ("dp", "x", "zh", "y", "core"))
    time = ("x", "zh", "y", "core")
    wide = P("dp", time, None)
    return jax.shard_map(
        shards,
        mesh=fine,
        in_specs=(
            wide,
            wide,
            wide,
            P("dp", time),
            P("dp", time),
            wide,
            wide,
            P(("y", "core"), ("x", "zh"), "dp"),
            P(("y", "core"), "dp", ("x", "zh")),
            wide,
        ),
        out_specs=(wide, wide, wide, wide),
        check_vma=False,
    )
```
